256 devices in a mesh: dp: 32 (over z_hi, y, core), tensor: 8 (over x, z_lo).
Axes of the slice: x: 4, y: 4, z: 8 (z_hi: 4, z_lo: 2; z = z_hi * 2 + z_lo), core: 2. Of those that a mesh axis runs over, the one named last changes fastest.
Arguments:
- hidden: bfloat16 [8192, 8192], P('dp', 'tensor'), may hold values from -6 to 6
- hidden_q: bfloat16 [8192, 8192], P('dp', 'tensor'), may hold values from -6 to 6
- norm_gain: float32 [8192], replicated, may hold values from 0.5 to 9
- doc_ids: int32 [64, 128], P('dp'), may hold values from 0 to 3, never falling along the last dimension, each value on 1 to 64 neighbouring positions
- w_query: bfloat16 [8192, 8192], P('dp', 'tensor'), may hold values from -0.0625 to 0.0625
- w_key: bfloat16 [8192, 1024], P(None, 'tensor'), may hold values from -0.0625 to 0.0625
- w_value: bfloat16 [8192, 1024], P(None, 'tensor'), may hold values from -0.0625 to 0.0625
Outputs:
- band_gram: float32 [256, 8192], P('dp', 'tensor')
- band_delta: float32 [256, 8192], P('dp', 'tensor')
- head_gram: float32 [8, 1024, 1024], P('tensor', 'dp')
- head_delta: float32 [8, 1024, 1024], P('tensor', 'dp')
The draws below stay inside these ranges and needn't reach their ends.
Inputs may be any that keep to these rules, and one draw needn't show every extreme that they name: `doc_ids`: document numbers never fall along a sequence; a document spans 1 to 64 positions, one exactly 64.
All inputs are finite; a program needn't handle non-finite values.
Results may differ from the reference program's by a relative error of at most 0.014.
Values may be sent and summed in bfloat16 or wider, within the bound.
No kernel may reach another device: no remote copies, remote signals or barrier semaphores. Data moves between devices by JAX's collectives and lax.ppermute only.
A program may use at most 128 MiB of HBM per device.

```python
import math
import jax
import jax.numpy as jnp
import numpy as np
from jax import lax

D = 8192
HS = 128
QH_DEV = 8
LEN = 128
BAND = 256
SEQS = 64
TOKENS = 8192
KV_HEADS = 8
HEADS = 64


def draw_norm_gain(key, part):
    key = jax.random.fold_in(key, 7)
    return jax.random.uniform(key, (D,), jnp.float32, 0.5, 1.5)


def block_levels(key, shape, cuts, least, largest):
    def one(position, shards_of):
        draws = jax.random.uniform(jax.random.fold_in(jax.random.fold_in(key, 6), position), (shards_of,), jnp.float32, least / len(cuts), largest / len(cuts))
        return jnp.repeat(jnp.exp(draws), shape[position] // shards_of).reshape((-1,) + (1,) * (len(shape) - position - 1))

    loudness = one(*cuts[0])
    for cut in cuts[1:]:
        loudness = loudness * one(*cut)
    return loudness


def profile(amount, total, reach, slope):
    portions = [(1 << 20) // math.isqrt(standing ** slope) + 1 for standing in range(2, amount + 1)]
    spare, counts = total - reach - (amount - 1), [1] * (amount - 1)
    while spare > 0:
        movable = [i for i in range(amount - 1) if counts[i] < reach]
        pool, budget = sum([portions[i] for i in movable]), spare
        for i in movable:
            addition = min(reach - counts[i], max(1, budget * portions[i] // pool), spare)
            counts[i] = counts[i] + addition
            spare = spare - addition
    return np.array([reach] + counts)


def ragged(stream_key, count, total, limit, skew):
    if count == 2:
        one = jax.random.randint(stream_key, (), max(1, total - limit), min(limit, total - 1) + 1)
        return jnp.stack([one, total - one])
    tallies = jnp.asarray(profile(count, total, limit, skew), jnp.int32)
    pairs = (count - 1) // 2
    giver, receiver = tallies[1:1 + 2 * pairs:2], tallies[2:2 + 2 * pairs:2]
    room = jnp.minimum(giver - 1, limit - receiver)
    shifted = jax.random.randint(jax.random.fold_in(stream_key, 1), (pairs,), 0, 1 << 20) % (room + 1)
    tallies = tallies.at[1:1 + 2 * pairs:2].set(giver - shifted).at[2:2 + 2 * pairs:2].set(receiver + shifted)
    return tallies[jax.random.permutation(jax.random.fold_in(stream_key, 2), count)]


def scatter_about(own_key, extent, deviation, reach, split=(), kind=jnp.bfloat16):
    drawn = deviation * jax.random.normal(own_key, extent, jnp.float32)
    if split:
        drawn = drawn * block_levels(own_key, extent, split, -0.22, 0.18)
    return jnp.clip(drawn, -reach, reach).astype(kind)


def setup_inputs(seed: int = 0) -> dict:
    arg_keys = jax.random.split(jax.random.key(seed), 8)
    hidden = scatter_about(arg_keys[0], (TOKENS, D), 1.0, 6.0, ((0, 32), (1, 8)))
    hidden_q = scatter_about(arg_keys[1], (TOKENS, D), 1.0, 6.0, ((0, 32), (1, 8)))
    norm_gain = draw_norm_gain(jax.random.fold_in(arg_keys[7], 71), 0)
    doc_ids = jax.vmap(lambda own: jnp.searchsorted(jnp.cumsum(ragged(own, 4, LEN, LEN // 2, 0)), jnp.arange(LEN), side="right"))(jax.random.split(arg_keys[3], SEQS)).reshape((SEQS, LEN)).astype(jnp.int32)
    w_query = scatter_about(arg_keys[4], (D, HEADS * HS), D ** -0.5, 0.0625, ((0, 32), (1, 8)))
    w_key = scatter_about(arg_keys[5], (D, KV_HEADS * HS), D ** -0.5, 0.0625, ((1, 8),))
    w_value = scatter_about(arg_keys[6], (D, KV_HEADS * HS), D ** -0.5, 0.0625, ((1, 8),))
    return {"hidden": hidden, "hidden_q": hidden_q, "norm_gain": norm_gain, "doc_ids": doc_ids, "w_query": w_query, "w_key": w_key, "w_value": w_value}


epsilon = 1e-05
rope_base = 500000.0

def rms_scale(values, norm_gain):
    widened = values.astype(jnp.float32)
    mean_square = lax.optimization_barrier(jnp.mean(widened * widened, axis=1, keepdims=True))
    return (widened * lax.rsqrt(mean_square + epsilon) * norm_gain[None, :]).astype(jnp.bfloat16)

def apply_rope(values):
    length = values.shape[-3]
    head_size = values.shape[-1]
    half_size = head_size // 2
    frequency = rope_base ** (-jnp.arange(half_size, dtype=jnp.float32) * 2.0 / head_size)
    angles = jnp.arange(length, dtype=jnp.float32)[:, None] * frequency[None, :]
    cosine = jnp.cos(angles)[:, None, :]
    sine_table = jnp.sin(angles)[:, None, :]
    first_half = values[..., :half_size]
    second_half = values[..., half_size:]
    return jnp.concatenate([first_half * cosine - second_half * sine_table, second_half * cosine + first_half * sine_table], axis=-1)

def stream_attention(normed_in, doc_ids, w_query, w_key, w_value):
    kv_count = w_key.shape[1] // HS
    queries = jnp.dot(normed_in, w_query, preferred_element_type=jnp.float32)
    queries = apply_rope(queries.reshape(SEQS, LEN, kv_count * QH_DEV, HS)).astype(jnp.bfloat16)
    queries = queries.reshape(SEQS, LEN, kv_count, QH_DEV, HS)
    key_rows = jnp.dot(normed_in, w_key, preferred_element_type=jnp.float32)
    key_rows = apply_rope(key_rows.reshape(SEQS, LEN, kv_count, HS)).astype(jnp.bfloat16)
    value_rows = jnp.dot(normed_in, w_value, preferred_element_type=jnp.float32).astype(jnp.bfloat16)
    value_rows = value_rows.reshape(SEQS, LEN, kv_count, HS)
    scaling = HS ** (-0.5)
    scores = jnp.einsum('sqghe,skge->sghqk', queries.astype(jnp.float32), key_rows.astype(jnp.float32)) * scaling
    row_index = jnp.arange(LEN)[:, None]
    col_index = jnp.arange(LEN)[None, :]
    allowed = (doc_ids[:, :, None] == doc_ids[:, None, :]) & (col_index <= row_index)[None]
    scores = jnp.where(allowed[:, None, None], scores, -1e+30)
    row_max = lax.optimization_barrier(jnp.max(scores, axis=-1, keepdims=True))
    exponent = jnp.exp(scores - row_max)
    weights = (exponent / lax.optimization_barrier(jnp.sum(exponent, axis=-1, keepdims=True))).astype(jnp.bfloat16)
    attended = jnp.einsum('sghqk,skge->sqghe', weights.astype(jnp.float32), value_rows.astype(jnp.float32))
    return attended.astype(jnp.bfloat16).reshape(TOKENS, kv_count, QH_DEV * HS)

def reference(hidden, hidden_q, norm_gain, doc_ids, w_query, w_key, w_value):
    normed = rms_scale(hidden, norm_gain)
    normed_q = rms_scale(hidden_q, norm_gain)
    attended = stream_attention(normed, doc_ids, w_query, w_key, w_value)
    attended_q = stream_attention(normed_q, doc_ids, w_query, w_key, w_value)
    band_diff = (normed[:, :BAND].astype(jnp.float32) - normed_q[:, :BAND].astype(jnp.float32)).astype(jnp.bfloat16)
    band_gram = jnp.dot(normed_q[:, :BAND].T, normed_q, preferred_element_type=jnp.float32) / TOKENS
    band_delta = jnp.dot(band_diff.T, normed_q, preferred_element_type=jnp.float32) / TOKENS
    head_diff = (attended.astype(jnp.float32) - attended_q.astype(jnp.float32)).astype(jnp.bfloat16)
    head_gram = jnp.einsum('rgi,rgj->gij', attended_q.astype(jnp.float32), attended_q.astype(jnp.float32)) / TOKENS
    head_delta = jnp.einsum('rgi,rgj->gij', head_diff.astype(jnp.float32), attended_q.astype(jnp.float32)) / TOKENS
    return (band_gram, band_delta, head_gram, head_delta)
```

```python
import functools

import jax
import jax.numpy as jnp
from jax import lax
from jax.experimental import pallas as pl
from jax.experimental.pallas import tpu as pltpu
from jax.sharding import PartitionSpec as P

HS = 128
QH = 8
LEN = 128
BAND = 256
WIDTH = 1024
TOKENS = 8192
EPS = 1e-05
ROPE_BASE = 500000.0
BF = jnp.bfloat16
F32 = jnp.float32

SIZES = {"zh": 4, "y": 4, "c": 2, "x": 4, "zl": 2}
STRIDES = {"zh": 64, "y": 16, "c": 8, "x": 2, "zl": 1}


def shift(value, axis, step):
    size, stride = SIZES[axis], STRIDES[axis]
    pairs = []
    for index in range(256):
        at = index // stride % size
        pairs.append((index, index + ((at + step) % size - at) * stride))
    return lax.ppermute(value, ("dp", "tensor"), pairs)


def take(value, index, axis):
    return lax.dynamic_index_in_dim(value, index, axis, keepdims=False)


def params(mib):
    return pltpu.CompilerParams(vmem_limit_bytes=mib * 2**20)


def cost(flops, moved):
    return pl.CostEstimate(flops=flops, bytes_accessed=moved, transcendentals=0)


def prepare_kernel(core, q_keep, q_give, f_keep, f_give, keep_ref, give_ref):
    keep_ref[0, :256] = q_keep[...]
    keep_ref[0, 256:] = f_keep[...]
    give_ref[0, :256] = q_give[...]
    give_ref[0, 256:] = f_give[...]


def prepare(core, hidden_q, hidden):
    own = pl.BlockSpec((256, 256), lambda b, c: (0, 2 * b + c[0]))
    other = pl.BlockSpec((256, 256), lambda b, c: (0, 2 * b + 1 - c[0]))
    out = pl.BlockSpec((1, 512, 256), lambda b, c: (b, 0, 0))
    return pl.pallas_call(
        prepare_kernel,
        grid_spec=pltpu.PrefetchScalarGridSpec(
            num_scalar_prefetch=1,
            grid=(2,),
            in_specs=[own, other, own, other],
            out_specs=[out, out],
        ),
        out_shape=[jax.ShapeDtypeStruct((2, 512, 256), BF)] * 2,
        compiler_params=params(8),
        cost_estimate=cost(0, 2**21),
    )(core, hidden_q, hidden_q, hidden, hidden)


def project_kernel(core, s_ref, w_ref, k_ref, v_ref, own_ref, sib_ref, acc):
    step = pl.program_id(0)
    w = w_ref[...].reshape(1024, WIDTH)
    kv = jnp.concatenate(
        [k_ref[...].reshape(1024, HS), v_ref[...].reshape(1024, HS)], axis=1
    )
    for tile in range(4):
        rows = pl.ds(tile * 256, 256)
        s = jnp.concatenate([s_ref[part, rows, :] for part in range(4)], axis=1)
        wide = jnp.dot(s, w, preferred_element_type=F32)
        narrow = jnp.dot(s, kv, preferred_element_type=F32)

        @pl.when(step == 0)
        def _():
            acc[rows, :WIDTH] = wide
            acc[rows, WIDTH:] = narrow

        @pl.when(step > 0)
        def _():
            acc[rows, :WIDTH] += wide
            acc[rows, WIDTH:] += narrow

    @pl.when(step == 3)
    def _():
        own_ref[...] = acc[:512]
        sib_ref[...] = acc[512:].astype(BF)


def project(core, normed, weights, w_key, w_value):
    narrow = pl.BlockSpec((1, 4, 1, 256, HS), lambda k, c: (k, 0, c[0], 0, 0))
    out = pl.BlockSpec((512, 1280), lambda k, c: (0, 0))
    return pl.pallas_call(
        project_kernel,
        grid_spec=pltpu.PrefetchScalarGridSpec(
            num_scalar_prefetch=1,
            grid=(4,),
            in_specs=[
                pl.BlockSpec((4, 1024, 256), lambda k, c: (k, 0, 0)),
                pl.BlockSpec((4, 256, WIDTH), lambda k, c: (k, 0, 0)),
                narrow,
                narrow,
            ],
            out_specs=[out, out],
            scratch_shapes=[pltpu.VMEM((1024, 1280), F32)],
        ),
        out_shape=[
            jax.ShapeDtypeStruct((512, 1280), F32),
            jax.ShapeDtypeStruct((512, 1280), BF),
        ],
        compiler_params=params(32),
        cost_estimate=cost(2 * 1024 * 4096 * 1280, 24 * 2**20),
    )(
        core,
        normed,
        weights,
        w_key.reshape(4, 4, 2, 256, HS),
        w_value.reshape(4, 4, 2, 256, HS),
    )


def rope_tables():
    half = HS // 2
    frequency = ROPE_BASE ** (-jnp.arange(half, dtype=F32) * 2.0 / HS)
    angles = jnp.arange(LEN, dtype=F32)[:, None] * frequency[None, :]
    cosine, sine = jnp.cos(angles), jnp.sin(angles)
    return jnp.concatenate([cosine, cosine], 1), jnp.concatenate([-sine, sine], 1)


def attended_columns(own_ref, got_ref, col_ref, row_ref, cos_ref, sin_ref):
    cosine, sine = cos_ref[...], sin_ref[...]

    def columns(at):
        cols = pl.ds(at * HS, HS)
        return own_ref[0, 0, :, cols] + got_ref[0, 0, :, cols].astype(F32)

    def rotate(block):
        return (block * cosine + pltpu.roll(block, HS // 2, 1) * sine).astype(BF)

    keys = rotate(columns(QH))
    values = columns(QH + 1).astype(BF)
    row = lax.broadcasted_iota(jnp.int32, (LEN, LEN), 0)
    col = lax.broadcasted_iota(jnp.int32, (LEN, LEN), 1)
    allowed = (col_ref[0] == row_ref[0]) & (col <= row)
    nt = (((1,), (1,)), ((), ()))
    blocks = []
    for head in range(QH):
        scores = lax.dot_general(rotate(columns(head)), keys, nt, preferred_element_type=F32)
        scores = jnp.where(allowed, scores * HS ** (-0.5), -1e30)
        exponent = jnp.exp(scores - jnp.max(scores, axis=-1, keepdims=True))
        weights = (exponent / jnp.sum(exponent, axis=-1, keepdims=True)).astype(BF)
        blocks.append(
            lax.dot_general(
                values, weights, (((0,), (1,)), ((), ())), preferred_element_type=F32
            ).astype(BF)
        )
    return blocks


def attend_kernel(own_ref, got_ref, col_ref, row_ref, cos_ref, sin_ref, out_ref):
    blocks = attended_columns(own_ref, got_ref, col_ref, row_ref, cos_ref, sin_ref)
    for head, block in enumerate(blocks):
        out_ref[pl.ds(head * HS, HS), :] = block


def attend_diff_kernel(
    core, own_ref, got_ref, col_ref, row_ref, cos_ref, sin_ref, q_ref, keep_ref, give_ref
):
    blocks = attended_columns(own_ref, got_ref, col_ref, row_ref, cos_ref, sin_ref)
    first = core[0] == 0
    for head, block in enumerate(blocks):
        diff = block.astype(F32) - q_ref[pl.ds(head * HS, HS), :].astype(F32)
        diff = diff.reshape(2, 2, 32, LEN)
        keep_ref[pl.ds(head * 2, 2)] = jnp.where(first, diff[:, 0], diff[:, 1]).astype(BF)
        give_ref[pl.ds(head * 2, 2)] = jnp.where(first, diff[:, 1], diff[:, 0]).astype(BF)


def attend(own_rows, got_rows, ids, tables):
    rows = pl.BlockSpec((1, 1, LEN, 1280), lambda s: (0, s, 0, 0))
    table = pl.BlockSpec((LEN, HS), lambda s: (0, 0))
    return pl.pallas_call(
        attend_kernel,
        grid=(2,),
        in_specs=[
            rows,
            rows,
            pl.BlockSpec((1, LEN, 1), lambda s: (s, 0, 0)),
            pl.BlockSpec((1, 1, LEN), lambda s: (s, 0, 0)),
            table,
            table,
        ],
        out_specs=pl.BlockSpec((WIDTH, LEN), lambda s: (0, s)),
        out_shape=jax.ShapeDtypeStruct((WIDTH, 256), BF),
        compiler_params=params(16),
        cost_estimate=cost(2**27, 2**21),
    )(own_rows, got_rows, ids[:, :, None], ids[:, None, :], *tables)


def attend_diff(core, own_rows, got_rows, ids, tables, att_q):
    rows = pl.BlockSpec((1, 1, LEN, 1280), lambda s, c: (1, s, 0, 0))
    table = pl.BlockSpec((LEN, HS), lambda s, c: (0, 0))
    half = pl.BlockSpec((16, 32, LEN), lambda s, c: (0, 0, s))
    return pl.pallas_call(
        attend_diff_kernel,
        grid_spec=pltpu.PrefetchScalarGridSpec(
            num_scalar_prefetch=1,
            grid=(2,),
            in_specs=[
                rows,
                rows,
                pl.BlockSpec((1, LEN, 1), lambda s, c: (s, 0, 0)),
                pl.BlockSpec((1, 1, LEN), lambda s, c: (s, 0, 0)),
                table,
                table,
                pl.BlockSpec((WIDTH, LEN), lambda s, c: (0, s)),
            ],
            out_specs=[half, half],
        ),
        out_shape=[jax.ShapeDtypeStruct((16, 32, 256), BF)] * 2,
        compiler_params=params(16),
        cost_estimate=cost(2**27, 2**21),
    )(core, own_rows, got_rows, ids[:, :, None], ids[:, None, :], *tables, att_q)


def moments_kernel(place, left_ref, left_sib_ref, right_ref, right_sib_ref, out_ref):
    nt = (((1,), (1,)), ((), ()))
    left = left_ref[...].reshape(128, 256)
    left_sib = left_sib_ref[...].reshape(128, 256)
    total = lax.dot_general(left, right_ref[...], nt, preferred_element_type=F32)
    total += lax.dot_general(left_sib, right_sib_ref[...], nt, preferred_element_type=F32)
    out_ref[0] = total.astype(BF).reshape(4, 32, WIDTH)


def moments(place, left, left_sib, right, right_sib):
    def side(value):
        if value.shape[0] == 16:
            value = value.reshape(4, 4, 1, 32, 256)
            at = lambda d, p: (0, (p[1] + d) % 4, 0, 0, 0)
        else:
            value = value.reshape(4, 4, 2, 32, 256)
            at = lambda d, p: (0, (p[1] + d) % 4, p[0], 0, 0)
        return value, pl.BlockSpec((4, 1, 1, 32, 256), at)

    left, left_spec = side(left)
    left_sib, left_sib_spec = side(left_sib)
    whole = pl.BlockSpec((WIDTH, 256), lambda d, p: (0, 0))
    return pl.pallas_call(
        moments_kernel,
        grid_spec=pltpu.PrefetchScalarGridSpec(
            num_scalar_prefetch=1,
            grid=(4,),
            in_specs=[left_spec, left_sib_spec, whole, whole],
            out_specs=pl.BlockSpec((1, 4, 32, WIDTH), lambda d, p: (d, 0, 0, 0)),
        ),
        out_shape=jax.ShapeDtypeStruct((4, 4, 32, WIDTH), BF),
        compiler_params=params(16),
        cost_estimate=cost(2**30, 2**21),
    )(place, left, left_sib, right, right_sib)


def band_kernel(place, lead_ref, lead_got_ref, right_ref, out_ref):
    first = place[0] == 0
    tn = (((0,), (0,)), ((), ()))
    gram = jnp.zeros((256, 256), F32)
    delta = jnp.zeros((256, 256), F32)
    for owner in range(2):
        lead_q = jnp.where(first, lead_ref[owner, 0], lead_got_ref[1 - owner, 0])
        lead_f = jnp.where(first, lead_ref[owner, 1], lead_got_ref[1 - owner, 1])
        diff = (lead_f.astype(F32) - lead_q.astype(F32)).astype(BF)
        right = right_ref[0, owner, 0]
        gram += lax.dot_general(lead_q, right, tn, preferred_element_type=F32)
        delta += lax.dot_general(diff, right, tn, preferred_element_type=F32)
    out_ref[0] = gram.astype(BF)
    out_ref[1] = delta.astype(BF)


def band_moments(place, lead, lead_got, normed):
    whole = pl.BlockSpec((2, 2, 256, 256), lambda b, p: (0, 0, 0, 0))
    return pl.pallas_call(
        band_kernel,
        grid_spec=pltpu.PrefetchScalarGridSpec(
            num_scalar_prefetch=1,
            grid=(2,),
            in_specs=[
                whole,
                whole,
                pl.BlockSpec((1, 2, 1, 256, 256), lambda b, p: (2 * p[1] + b, 0, 0, 0, 0)),
            ],
            out_specs=pl.BlockSpec((2, 256, 256), lambda b, p: (0, 0, b)),
        ),
        out_shape=jax.ShapeDtypeStruct((2, 256, 512), BF),
        compiler_params=params(16),
        cost_estimate=cost(2**29, 2**21),
    )(
        place,
        lead.reshape(2, 2, 256, 256),
        lead_got.reshape(2, 2, 256, 256),
        normed.reshape(16, 2, 2, 256, 256),
    )


def scatter(parts, axis, here):
    total = take(parts, here, 0).astype(F32)
    for step in (1, 3, 2):
        total = total + shift(take(parts, (here + step) % 4, 0), axis, step).astype(F32)
    return total


def near(value, axis):
    return shift(value, axis, 1), shift(value, axis, -1)


def far(below, above, axis):
    half = below.shape[0] // 2
    return shift(below[:half], axis, 1), shift(above[half:], axis, -1)


def stage(*values):
    return lax.optimization_barrier(values)


def local(hidden, hidden_q, norm_gain, doc_ids, w_query, w_key, w_value):
    dp, tensor = lax.axis_index("dp"), lax.axis_index("tensor")
    zh, y, c = dp // 8, dp // 2 % 4, dp % 2
    x, zl = tensor // 2, tensor % 2
    core = c.reshape(1)

    z1 = near(w_query, "zh")
    y1 = near(w_query, "y")
    keep, give = prepare(core, hidden_q, hidden)
    got = shift(give, "c", 1)
    piece = jnp.concatenate([keep, got], 1)
    x1 = near(piece, "x")

    both = jnp.concatenate([hidden_q, hidden])
    squares = jnp.sum(jnp.square(both.astype(F32)), axis=-1)
    squares = squares + shift(squares, "x", 1) + shift(squares, "x", 2) + shift(squares, "x", 3)
    squares = squares + shift(squares, "zl", 1)
    squares = jnp.concatenate([squares, shift(squares, "c", 1)])

    y1a, y1b, w_query, piece = stage(*y1, w_query, piece)
    yf = far(y1a, y1b, "y")
    z1a, z1b, yfa, yfb, piece, x1a, x1b = stage(*z1, *yf, piece, *x1)
    pair = jnp.concatenate([z1a, z1b])
    py1 = near(pair, "y")
    other = shift(piece, "zl", 1)
    xf = far(x1a, x1b, "x")
    xfa, xfb, other, z1a, z1b = stage(*xf, other, z1a, z1b)
    ox1 = near(other, "x")
    zf = far(z1a, z1b, "zh")
    py1a, py1b, zfa, zfb = stage(*py1, *zf)
    distant = jnp.concatenate([zfa, zfb])
    pyf = (
        shift(py1a.reshape(2, 256, WIDTH)[:, :128].reshape(256, WIDTH), "y", 1),
        shift(py1b.reshape(2, 256, WIDTH)[:, 128:].reshape(256, WIDTH), "y", -1),
    )
    dy1 = near(distant, "y")
    ox1a, ox1b, pyfa, pyfb = stage(*ox1, *pyf)
    oxf = far(ox1a, ox1b, "x")
    dy1a, dy1b, pyfa = stage(*dy1, pyfa)
    dyf = far(dy1a, dy1b, "y")

    scale = lax.rsqrt(squares / 8192.0 + EPS)[:, None]
    gain = take(norm_gain.reshape(4, 2, 2, 2, 256), c, 3)
    normed = jnp.zeros((16, 1024, 256), BF)
    for dz, blocks in (
        (0, ((0, 0, piece), (-1, 0, x1a), (1, 0, x1b), (2, 0, xfa), (2, 1, xfb))),
        (1, ((0, 0, other), (-1, 0, ox1a), (1, 0, ox1b), (2, 0, oxf[0]), (2, 1, oxf[1]))),
    ):
        at_zl = (zl + dz) % 2
        for dx, part, block in blocks:
            at_x = (x + dx) % 4
            own_gain = take(take(gain, at_x, 0), at_zl, 0)[part : part + block.shape[0], None, :]
            block = (block.astype(F32) * scale[None] * own_gain).astype(BF)
            normed = lax.dynamic_update_slice(normed, block, (at_x * 4 + at_zl * 2 + part, 0, 0))

    weights = jnp.zeros((16, 256, WIDTH), BF)
    rows = [(0, 0, 0, w_query), (0, -1, 0, y1a), (0, 1, 0, y1b), (0, 2, 0, yfa), (0, 2, 1, yfb)]
    for part, dz in enumerate((-1, 1)):
        half, whole = slice(part * 128, part * 128 + 128), slice(part * 256, part * 256 + 256)
        rows += [
            (dz, 0, 0, pair[whole]),
            (dz, -1, 0, py1a[whole]),
            (dz, 1, 0, py1b[whole]),
            (dz, 2, 0, pyfa[half]),
            (dz, 2, 1, pyfb[half]),
        ]
    rows += [(2, 0, 0, distant), (2, -1, 0, dy1a), (2, 1, 0, dy1b)]
    rows += [(2, 2, 0, dyf[0]), (2, 2, 1, dyf[1])]
    for dz, dy, part, block in rows:
        at = (zh + dz) % 4 * 4 + (y + dy) % 4
        weights = lax.dynamic_update_slice(weights, block[None], (at, part * 128, 0))

    own_rows, sib_rows = project(core, normed, weights, w_key, w_value)
    own_rows = own_rows.reshape(2, 2, LEN, 1280)
    got_rows = shift(sib_rows, "c", 1).reshape(2, 2, LEN, 1280)
    tables = rope_tables()
    att_q = attend(own_rows, got_rows, doc_ids, tables)
    att_sib = shift(att_q, "c", 1)
    keep, give = attend_diff(core, own_rows, got_rows, doc_ids, tables, att_q)
    keep_sib = shift(give, "c", 1)
    place = jnp.stack([c, y])
    outs = []
    for left, left_sib in ((att_q, att_sib), (keep, keep_sib)):
        sums = moments(place, left, left_sib, att_q, att_sib)
        total = sums[0].astype(F32)
        for step in (1, 3, 2):
            total = total + shift(sums[step], "y", step).astype(F32)
        outs.append((scatter(total.astype(BF), "zh", zh) / TOKENS)[None])

    lead = normed[0]
    band = band_moments(jnp.stack([c, tensor]), lead, shift(lead, "c", 1), normed)
    band = band.reshape(2, 4, 4, 16, 512)
    band = scatter(band.transpose(2, 1, 0, 3, 4), "y", y).astype(BF)
    band = scatter(band, "zh", zh).reshape(2, 2, 8, 2, 256) / TOKENS
    other = shift(take(band, 1 - c, 1), "c", 1)
    mine = take(band, c, 1)
    band = jnp.stack(
        [jnp.where(c == 0, mine, other), jnp.where(c == 0, other, mine)], 3
    ).reshape(2, 8, WIDTH)
    return band[0], band[1], outs[0], outs[1]


def solution(mesh):
    return jax.shard_map(
        local,
        mesh=mesh,
        in_specs=(
            P("dp", "tensor"),
            P("dp", "tensor"),
            P(),
            P("dp", None),
            P("dp", "tensor"),
            P(None, "tensor"),
            P(None, "tensor"),
        ),
        out_specs=(
            P("dp", "tensor"),
            P("dp", "tensor"),
            P("tensor", "dp", None),
            P("tensor", "dp", None),
        ),
        check_vma=False,
    )
```

```python
import functools

import functools

import jax
import jax.numpy as jnp
from jax import lax
from jax.experimental import pallas as pl
from jax.experimental.pallas import tpu as pltpu
from jax.sharding import PartitionSpec as P

HS = 128
QH = 8
LEN = 128
BAND = 256
WIDTH = 1024
TOKENS = 8192
EPS = 1e-05
ROPE_BASE = 500000.0
BF = jnp.bfloat16
F32 = jnp.float32

SIZES = {"zh": 4, "y": 4, "c": 2, "x": 4, "zl": 2}
STRIDES = {"zh": 64, "y": 16, "c": 8, "x": 2, "zl": 1}


def shift(value, axis, step):
    size, stride = SIZES[axis], STRIDES[axis]
    pairs = []
    for index in range(256):
        at = index // stride % size
        pairs.append((index, index + ((at + step) % size - at) * stride))
    return lax.ppermute(value, ("dp", "tensor"), pairs)


def turn(value, axis, step):
    size, stride = SIZES[axis], STRIDES[axis]
    pairs = []
    for index in range(256):
        at = index // stride % size
        own = -step if index // STRIDES["c"] % 2 else step
        pairs.append((index, index + ((at + own) % size - at) * stride))
    return lax.ppermute(value, ("dp", "tensor"), pairs)


def take(value, index, axis):
    return lax.dynamic_index_in_dim(value, index, axis, keepdims=False)


def params(mib):
    return pltpu.CompilerParams(vmem_limit_bytes=mib * 2**20)


def cost(flops, moved):
    return pl.CostEstimate(flops=flops, bytes_accessed=moved, transcendentals=0)


def prepare_kernel(core, q_keep, q_give, f_keep, f_give, keep_ref, give_ref):
    keep_ref[0, :256] = q_keep[...]
    keep_ref[0, 256:] = f_keep[...]
    give_ref[0, :256] = q_give[...]
    give_ref[0, 256:] = f_give[...]


def prepare(core, hidden_q, hidden):
    own = pl.BlockSpec((256, 256), lambda b, c: (0, 2 * b + c[0]))
    other = pl.BlockSpec((256, 256), lambda b, c: (0, 2 * b + 1 - c[0]))
    out = pl.BlockSpec((1, 512, 256), lambda b, c: (b, 0, 0))
    return pl.pallas_call(
        prepare_kernel,
        grid_spec=pltpu.PrefetchScalarGridSpec(
            num_scalar_prefetch=1,
            grid=(2,),
            in_specs=[own, other, own, other],
            out_specs=[out, out],
        ),
        out_shape=[jax.ShapeDtypeStruct((2, 512, 256), BF)] * 2,
        compiler_params=params(8),
        cost_estimate=cost(0, 2**21),
    )(core, hidden_q, hidden_q, hidden, hidden)


def project_kernel(half, at, *refs):
    s_refs, w_refs = refs[:8], refs[8:20]
    k_ref, v_ref, scale_ref, gain_ref, out_ref, lead_ref, right_ref = refs[20:27]
    s_buf, w_buf, acc, s_sem, w_sem = refs[27:]
    total = out_ref if half == 0 else acc
    for index, ref in enumerate(s_refs):
        slot = at[2 + index]
        rows = ref.at[:, pl.ds(512 * half, 512)]
        pltpu.make_async_copy(rows, s_buf.at[slot], s_sem.at[slot]).start()
    index = 10
    for ref in w_refs:
        for part in range(ref.shape[0] // 256):
            slot = at[index]
            rows = ref.at[pl.ds(256 * part, 256)]
            pltpu.make_async_copy(rows, w_buf.at[slot], w_sem.at[slot]).start()
            index += 1

    def normed(slot, part, rows):
        block = s_buf[slot, part, rows, :].astype(F32)
        own_gain = gain_ref[pl.ds(2 * slot + part, 1), :]
        scale = scale_ref[rows, :]
        return (block * jnp.concatenate([scale, scale], 1) * own_gain).astype(BF)

    everything = pl.ds(0, 512)
    for step in range(4):
        for part in range(2):
            slot = 2 * step + part
            pltpu.make_async_copy(s_buf.at[slot], s_buf.at[slot], s_sem.at[slot]).wait()
        for part in range(4):
            slot = 4 * step + part
            pltpu.make_async_copy(w_buf.at[slot], w_buf.at[slot], w_sem.at[slot]).wait()
        w = w_buf[pl.ds(4 * step, 4)].reshape(1024, WIDTH)
        kv = jnp.concatenate(
            [k_ref[step].reshape(1024, HS), v_ref[step].reshape(1024, HS)], axis=1
        )
        s = jnp.concatenate(
            [normed(2 * step + part // 2, part % 2, everything) for part in range(4)], axis=1
        )
        wide = jnp.dot(s, w, preferred_element_type=F32)
        narrow = jnp.dot(s, kv, preferred_element_type=F32)
        if step == 0:
            total[:, :WIDTH] = wide
            total[:, WIDTH:] = narrow
            lead_ref[...] = s[:, :256]
        else:
            total[:, :WIDTH] += wide
            total[:, WIDTH:] += narrow

    for part in range(2):
        right_ref[part] = normed(at[1], part, pl.ds(0, 256))
    if half:
        out_ref[...] = acc[...].astype(BF)


def project(half, at, pieces, rows, w_key, w_value, scale, gain):
    whole = lambda *shape: pl.BlockSpec(shape, lambda i, at: (0,) * len(shape))
    narrow = pl.BlockSpec((4, 4, 1, 256, HS), lambda i, at: (0, 0, at[0], 0, 0))
    return pl.pallas_call(
        functools.partial(project_kernel, half),
        grid_spec=pltpu.PrefetchScalarGridSpec(
            num_scalar_prefetch=1,
            grid=(1,),
            in_specs=[pl.BlockSpec(memory_space=pltpu.HBM)] * 20
            + [narrow, narrow, whole(512, 128), whole(16, 256)],
            out_specs=[whole(512, 1280), whole(512, 256), whole(2, 256, 256)],
            scratch_shapes=[
                pltpu.VMEM((8, 2, 512, 256), BF),
                pltpu.VMEM((16, 256, WIDTH), BF),
                pltpu.VMEM((512, 1280) if half else (8, 128), F32),
                pltpu.SemaphoreType.DMA((8,)),
                pltpu.SemaphoreType.DMA((16,)),
            ],
        ),
        out_shape=[
            jax.ShapeDtypeStruct((512, 1280), BF if half else F32),
            jax.ShapeDtypeStruct((512, 256), BF),
            jax.ShapeDtypeStruct((2, 256, 256), BF),
        ],
        compiler_params=params(28),
        cost_estimate=cost(2 * 512 * 4096 * 1280, 16 * 2**20),
    )(
        at,
        *(pltpu.with_memory_space_constraint(v, pltpu.HBM) for v in pieces),
        *(pltpu.with_memory_space_constraint(v, pltpu.HBM) for v in rows),
        w_key.reshape(4, 4, 2, 256, HS),
        w_value.reshape(4, 4, 2, 256, HS),
        scale,
        gain,
    )


def rope_tables():
    half = HS // 2
    frequency = ROPE_BASE ** (-jnp.arange(half, dtype=F32) * 2.0 / HS)
    angles = jnp.arange(LEN, dtype=F32)[:, None] * frequency[None, :]
    cosine, sine = jnp.cos(angles), jnp.sin(angles)
    return jnp.concatenate([cosine, cosine], 1), jnp.concatenate([-sine, sine], 1)


def attended_columns(own_ref, got_ref, col_ref, row_ref, cos_ref, sin_ref):
    cosine, sine = cos_ref[...], sin_ref[...]

    def columns(at):
        cols = pl.ds(at * HS, HS)
        return own_ref[0, 0, :, cols] + got_ref[0, 0, :, cols].astype(F32)

    def rotate(block):
        return (block * cosine + pltpu.roll(block, HS // 2, 1) * sine).astype(BF)

    keys = rotate(columns(QH))
    values = columns(QH + 1).astype(BF)
    row = lax.broadcasted_iota(jnp.int32, (LEN, LEN), 0)
    col = lax.broadcasted_iota(jnp.int32, (LEN, LEN), 1)
    allowed = (col_ref[0] == row_ref[0]) & (col <= row)
    nt = (((1,), (1,)), ((), ()))
    queries = jnp.concatenate([rotate(columns(head)) for head in range(QH)], axis=0)
    scores = lax.dot_general(queries, keys, nt, preferred_element_type=F32) * HS ** (-0.5)
    scores = jnp.where(jnp.concatenate([allowed] * QH, axis=0), scores, -1e30)
    exponent = jnp.exp(scores - jnp.max(scores, axis=-1, keepdims=True))
    weights = (exponent / jnp.sum(exponent, axis=-1, keepdims=True)).astype(BF)
    attended = lax.dot_general(
        values, weights, (((0,), (1,)), ((), ())), preferred_element_type=F32
    ).astype(BF)
    return [attended[:, head * LEN : (head + 1) * LEN] for head in range(QH)]


def attend_kernel(own_ref, got_ref, col_ref, row_ref, cos_ref, sin_ref, out_ref):
    blocks = attended_columns(own_ref, got_ref, col_ref, row_ref, cos_ref, sin_ref)
    for head, block in enumerate(blocks):
        out_ref[pl.ds(head * HS, HS), :] = block


def attend_diff_kernel(
    core, own_ref, got_ref, col_ref, row_ref, cos_ref, sin_ref, q_ref, keep_ref, give_ref
):
    blocks = attended_columns(own_ref, got_ref, col_ref, row_ref, cos_ref, sin_ref)
    first = core[0] == 0
    for head, block in enumerate(blocks):
        diff = block.astype(F32) - q_ref[pl.ds(head * HS, HS), :].astype(F32)
        diff = diff.reshape(2, 2, 32, LEN)
        keep_ref[pl.ds(head * 2, 2)] = jnp.where(first, diff[:, 0], diff[:, 1]).astype(BF)
        give_ref[pl.ds(head * 2, 2)] = jnp.where(first, diff[:, 1], diff[:, 0]).astype(BF)


def attend(own_rows, got_rows, ids, tables):
    rows = pl.BlockSpec((1, 1, LEN, 1280), lambda s: (0, s, 0, 0))
    table = pl.BlockSpec((LEN, HS), lambda s: (0, 0))
    return pl.pallas_call(
        attend_kernel,
        grid=(2,),
        in_specs=[
            rows,
            rows,
            pl.BlockSpec((1, LEN, 1), lambda s: (s, 0, 0)),
            pl.BlockSpec((1, 1, LEN), lambda s: (s, 0, 0)),
            table,
            table,
        ],
        out_specs=pl.BlockSpec((WIDTH, LEN), lambda s: (0, s)),
        out_shape=jax.ShapeDtypeStruct((WIDTH, 256), BF),
        compiler_params=params(16),
        cost_estimate=cost(2**27, 2**21),
    )(own_rows, got_rows, ids[:, :, None], ids[:, None, :], *tables)


def attend_diff(core, own_rows, got_rows, ids, tables, att_q):
    rows = pl.BlockSpec((1, 1, LEN, 1280), lambda s, c: (1, s, 0, 0))
    table = pl.BlockSpec((LEN, HS), lambda s, c: (0, 0))
    half = pl.BlockSpec((16, 32, LEN), lambda s, c: (0, 0, s))
    return pl.pallas_call(
        attend_diff_kernel,
        grid_spec=pltpu.PrefetchScalarGridSpec(
            num_scalar_prefetch=1,
            grid=(2,),
            in_specs=[
                rows,
                rows,
                pl.BlockSpec((1, LEN, 1), lambda s, c: (s, 0, 0)),
                pl.BlockSpec((1, 1, LEN), lambda s, c: (s, 0, 0)),
                table,
                table,
                pl.BlockSpec((WIDTH, LEN), lambda s, c: (0, s)),
            ],
            out_specs=[half, half],
        ),
        out_shape=[jax.ShapeDtypeStruct((16, 32, 256), BF)] * 2,
        compiler_params=params(16),
        cost_estimate=cost(2**27, 2**21),
    )(core, own_rows, got_rows, ids[:, :, None], ids[:, None, :], *tables, att_q)


def moments_kernel(place, left_ref, left_sib_ref, right_ref, right_sib_ref, *refs):
    nt = (((1,), (1,)), ((), ()))
    out_ref = refs[-1]

    def rows(ref):
        parts = [ref[:, (place[1] + step) % 4, 0].reshape(128, 256) for step in range(4)]
        return jnp.concatenate(parts, axis=0)

    total = lax.dot_general(rows(left_ref), right_ref[...], nt, preferred_element_type=F32)
    total += lax.dot_general(
        rows(left_sib_ref), right_sib_ref[...], nt, preferred_element_type=F32
    )
    out_ref[:, :, :32] = total.astype(BF).reshape(4, 4, 32, WIDTH)
    if len(refs) == 2:
        for step in range(4):
            out_ref[step, :, 32:] = refs[0][:, (place[1] + step) % 4]


def moments(place, left, left_sib, right, right_sib, *more):
    def side(value):
        if value.shape[0] == 16:
            value = value.reshape(4, 4, 1, 32, 256)
            return value, pl.BlockSpec((4, 4, 1, 32, 256), lambda i, p: (0, 0, 0, 0, 0))
        value = value.reshape(4, 4, 2, 32, 256)
        return value, pl.BlockSpec((4, 4, 1, 32, 256), lambda i, p: (0, 0, p[0], 0, 0))

    left, left_spec = side(left)
    left_sib, left_sib_spec = side(left_sib)
    whole = pl.BlockSpec((WIDTH, 256), lambda i, p: (0, 0))
    rows = 48 if more else 32
    return pl.pallas_call(
        moments_kernel,
        grid_spec=pltpu.PrefetchScalarGridSpec(
            num_scalar_prefetch=1,
            grid=(1,),
            in_specs=[left_spec, left_sib_spec, whole, whole]
            + [pl.BlockSpec((4, 4, 16, WIDTH), lambda i, p: (0, 0, 0, 0))] * len(more),
            out_specs=pl.BlockSpec((4, 4, rows, WIDTH), lambda i, p: (0, 0, 0, 0)),
        ),
        out_shape=jax.ShapeDtypeStruct((4, 4, rows, WIDTH), BF),
        compiler_params=params(24),
        cost_estimate=cost(2**30, 2**21),
    )(place, left, left_sib, right, right_sib, *more)


def band_kernel(place, own_ref, sib_ref, got_own_ref, got_sib_ref, right_ref, right_sib_ref, out_ref):
    first = place[0] == 0
    tn = (((0,), (0,)), ((), ()))
    for part in range(2):
        gram = jnp.zeros((256, 256), F32)
        delta = jnp.zeros((256, 256), F32)
        for mine, got, right in (
            (own_ref, got_sib_ref, right_ref),
            (sib_ref, got_own_ref, right_sib_ref),
        ):
            lead = jnp.where(first, mine[...], got[...])
            lead_q, lead_f = lead[:256], lead[256:]
            diff = (lead_f.astype(F32) - lead_q.astype(F32)).astype(BF)
            gram += lax.dot_general(lead_q, right[part], tn, preferred_element_type=F32)
            delta += lax.dot_general(diff, right[part], tn, preferred_element_type=F32)
        for index, value in enumerate((gram, delta)):
            cols = pl.ds(index * 512 + part * 256, 256)
            out_ref[:, :, :, cols] = value.astype(BF).reshape(4, 4, 16, 256)


def band_moments(place, *sides):
    return pl.pallas_call(
        band_kernel,
        in_specs=[pl.BlockSpec(memory_space=pltpu.SMEM)]
        + [pl.BlockSpec(memory_space=pltpu.VMEM)] * 6,
        out_specs=pl.BlockSpec(memory_space=pltpu.VMEM),
        out_shape=jax.ShapeDtypeStruct((4, 4, 16, WIDTH), BF),
        compiler_params=params(16),
        cost_estimate=cost(2**29, 2**21),
    )(place, *sides)


def scatter(parts, axis, here):
    total = take(parts, here, 0).astype(F32)
    for step in (1, 3, 2):
        total = total + shift(take(parts, (here + step) % 4, 0), axis, step).astype(F32)
    return total


PLAN = {
    "s": [
        ("s1", "t0", "x", 1, 3.0),
        ("s2", "t1", "x", 2, 3.0),
        ("s3", "t2", "zl", 1, 3.0),
        ("s4", "t3", "c", 1, 1.0),
    ],
    "z": [
        ("zA", "w", "zh", 1, 10.5),
        ("zB", "w", "zh", -1, 10.5),
        ("l", "p", "zl", 1, 21.0),
        ("zF", "zA", "zh", 1, 10.5),
    ],
    "y": [
        (f"{block}.{name}", block if name != "F" else f"{block}.A", "y", step, length)
        for block, length in (("w", 5.3), ("pair", 10.5), ("zF", 5.3))
        for name, step in (("A", 1), ("B", -1), ("F", 1))
    ],
    "x": [
        (f"{block}.{name}", block if name != "F" else f"{block}.A", "x", step, 10.5)
        for block in ("p", "l")
        for name, step in (("A", 1), ("B", -1), ("F", 1))
    ],
}
MADE = [
    ("t1", ("t0", "s1"), jnp.add),
    ("t2", ("t1", "s2"), jnp.add),
    ("t3", ("t2", "s3"), jnp.add),
    ("pair", ("zA", "zB"), lambda a, b: jnp.concatenate([a, b])),
]
LIMIT = {"y": 2, "z": 1, "x": 2, "s": 1}
IN_FLIGHT = 5
ISSUE, LATENCY = 2.0, 2.0


def exchange(env, ready):
    queues = {axis: list(ops) for axis, ops in PLAN.items()}
    free = dict.fromkeys(queues, 0.0)
    ready = dict(ready)
    flying, now = [], 0.0
    while any(queues.values()) or flying:
        started = True
        while started and len(flying) < IN_FLIGHT:
            started = False
            for axis, queue in queues.items():
                busy = sum(1 for entry in flying if entry[1] == axis)
                if not queue or busy >= LIMIT[axis] or len(flying) >= IN_FLIGHT:
                    continue
                name, source, along, step, length = queue[0]
                if ready.get(source, 1e9) > now:
                    continue
                queue.pop(0)
                move = shift if axis == "s" or along == "zl" else turn
                env[name] = move(env[source], along, step)
                now += ISSUE
                free[axis] = max(now, free[axis]) + length
                flying.append((free[axis] + LATENCY, axis, name))
                started = True
        waits = [entry[0] for entry in flying]
        later = [at for at in ready.values() if now < at < 1e8]
        if later and (not waits or min(later) < min(waits)):
            now = min(later)
            continue
        entry = min(flying)
        flying.remove(entry)
        now = max(now, entry[0])
        ready[entry[2]] = now
        held = {entry[2]}
        for queue in queues.values():
            held |= {op[1] for op in queue if ready.get(op[1], 1e9) <= now}
        held = sorted(held)
        for name, value in zip(held, lax.optimization_barrier(tuple(env[n] for n in held))):
            env[name] = value
        for name, sources, make in MADE:
            if name not in env and all(ready.get(n, 1e9) <= now for n in sources):
                env[name] = make(*(env[n] for n in sources))
                ready[name] = now
    return env


def local(hidden, hidden_q, norm_gain, doc_ids, w_query, w_key, w_value):
    dp, tensor = lax.axis_index("dp"), lax.axis_index("tensor")
    zh, y, c = dp // 8, dp // 2 % 4, dp % 2
    x, zl = tensor // 2, tensor % 2
    sign = 1 - 2 * c

    keep, give = prepare(c.reshape(1), hidden_q, hidden)
    piece = jnp.concatenate([keep, shift(give, "c", 1)], 1)
    both = jnp.concatenate([hidden_q, hidden])
    both, give = lax.optimization_barrier((both, give))
    squares = jnp.sum(jnp.square(both.astype(F32)), axis=-1)
    env = {"w": w_query, "p": piece, "t0": squares}
    env = exchange(env, {"w": 0.0, "p": 9.0, "t0": 7.0})

    scale = lax.rsqrt(jnp.stack([env["t3"], env["s4"]]) / 8192.0 + EPS)
    scale = jnp.broadcast_to(scale[:, :, None], (2, 512, 128))
    gain = take(norm_gain.reshape(16, 2, 256), c, 1)
    steps = (("", 0), (".A", -sign), (".B", sign), (".F", 2))
    at = [c, tensor]
    for block, dz in (("p", 0), ("l", 1)):
        at += [(x + dx) % 4 * 2 + (zl + dz) % 2 for _, dx in steps]
    rows = []
    for block, places in (("w", (0,)), ("pair", (-sign, sign)), ("zF", (2,))):
        at += [(zh + dz) % 4 * 4 + (y + dy) % 4 for _, dy in steps for dz in places]
        rows += [env[block + name] for name, _ in steps]
    at = jnp.stack(at)
    pieces = [env[block + name] for block in ("p", "l") for name, _ in steps]

    sib_rows, lead_sib, right_sib = project(1, at, pieces, rows, w_key, w_value, scale[1], gain)
    got_rows = shift(sib_rows, "c", 1).reshape(2, 2, LEN, 1280)
    got_lead = shift(lead_sib, "c", 1)
    own_rows, lead, right = project(0, at, pieces, rows, w_key, w_value, scale[0], gain)
    own_rows = own_rows.reshape(2, 2, LEN, 1280)
    got_lead_sib = shift(lead, "c", 1)
    tables = rope_tables()
    place = jnp.stack([c, y])
    att_q = attend(own_rows, got_rows, doc_ids, tables)
    att_sib = shift(att_q, "c", 1)
    lead, att_q = lax.optimization_barrier((lead, att_q))
    band = band_moments(place, lead, lead_sib, got_lead_sib, got_lead, right, right_sib)
    keep, give = attend_diff(c.reshape(1), own_rows, got_rows, doc_ids, tables, att_q)
    keep_sib = shift(give, "c", 1)
    outs = []
    for left, left_sib, more in ((att_q, att_sib, (band,)), (keep, keep_sib, ())):
        sums = moments(place, left, left_sib, att_q, att_sib, *more)
        total = sums[0].astype(F32)
        for step in (1, 3, 2):
            total = total + shift(sums[step], "y", step).astype(F32)
        outs.append(scatter(total.astype(BF), "zh", zh) / TOKENS)

    band = outs[0][32:].reshape(2, 8, 2, 2, 256).transpose(2, 0, 1, 3, 4)
    other = shift(take(band, 1 - c, 1), "c", 1)
    mine = take(band, c, 1)
    band = jnp.stack(
        [jnp.where(c == 0, mine, other), jnp.where(c == 0, other, mine)], 3
    ).reshape(2, 8, WIDTH)
    return band[0], band[1], outs[0][None, :32], outs[1][None]


def solution(mesh):
    return jax.shard_map(
        local,
        mesh=mesh,
        in_specs=(
            P("dp", "tensor"),
            P("dp", "tensor"),
            P(),
            P("dp", None),
            P("dp", "tensor"),
            P(None, "tensor"),
            P(None, "tensor"),
        ),
        out_specs=(
            P("dp", "tensor"),
            P("dp", "tensor"),
            P("tensor", "dp", None),
            P("tensor", "dp", None),
        ),
        check_vma=False,
    )
```

```python
import functools

import functools

import jax
import jax.numpy as jnp
from jax import lax
from jax.experimental import pallas as pl
from jax.experimental.pallas import tpu as pltpu
from jax.sharding import PartitionSpec as P

HS = 128
QH = 8
LEN = 128
BAND = 256
WIDTH = 1024
TOKENS = 8192
EPS = 1e-05
ROPE_BASE = 500000.0
BF = jnp.bfloat16
F32 = jnp.float32

SIZES = {"zh": 4, "y": 4, "c": 2, "x": 4, "zl": 2}
STRIDES = {"zh": 64, "y": 16, "c": 8, "x": 2, "zl": 1}


def shift(value, axis, step):
    size, stride = SIZES[axis], STRIDES[axis]
    pairs = []
    for index in range(256):
        at = index // stride % size
        pairs.append((index, index + ((at + step) % size - at) * stride))
    return lax.ppermute(value, ("dp", "tensor"), pairs)


def turn(value, axis, step):
    size, stride = SIZES[axis], STRIDES[axis]
    pairs = []
    for index in range(256):
        at = index // stride % size
        own = -step if index // STRIDES["c"] % 2 else step
        pairs.append((index, index + ((at + own) % size - at) * stride))
    return lax.ppermute(value, ("dp", "tensor"), pairs)


def take(value, index, axis):
    return lax.dynamic_index_in_dim(value, index, axis, keepdims=False)


def params(mib):
    return pltpu.CompilerParams(vmem_limit_bytes=mib * 2**20)


def cost(flops, moved):
    return pl.CostEstimate(flops=flops, bytes_accessed=moved, transcendentals=0)


def prepare_kernel(core, q_ref, f_ref, keep_ref, give_ref):
    first = core[0] == 0
    ones = jnp.ones((8, WIDTH), BF)
    nt = (((1,), (1,)), ((), ()))
    terms = []
    for stream, ref in enumerate((q_ref, f_ref)):
        square = jnp.square(ref[...].astype(F32))
        high = square.astype(BF)
        low = (square - high.astype(F32)).astype(BF)
        total = lax.dot_general(ones, high, nt, preferred_element_type=F32)
        total += lax.dot_general(ones, low, nt, preferred_element_type=F32)
        for _ in range(3):
            term = total[:1].astype(BF).astype(F32)
            terms.append(term)
            total = total - term
        for part in range(2):
            even, odd = (ref[:, pl.ds(512 * part + 256 * k, 256)] for k in range(2))
            rows = pl.ds(256 * stream, 256)
            keep_ref[part, rows] = jnp.where(first, even, odd)
            give_ref[part, rows] = jnp.where(first, odd, even)
    extra = jnp.concatenate(terms + [jnp.zeros((10, 256), F32)], axis=0).astype(BF)
    for part in range(2):
        keep_ref[part, pl.ds(512, 16)] = extra
        give_ref[part, pl.ds(512, 16)] = extra


def prepare(core, hidden_q, hidden):
    return pl.pallas_call(
        prepare_kernel,
        in_specs=[pl.BlockSpec(memory_space=pltpu.SMEM)]
        + [pl.BlockSpec(memory_space=pltpu.VMEM)] * 2,
        out_specs=[pl.BlockSpec(memory_space=pltpu.VMEM)] * 2,
        out_shape=[jax.ShapeDtypeStruct((2, 528, 256), BF)] * 2,
        compiler_params=params(16),
        cost_estimate=cost(0, 2**21),
    )(core, hidden_q, hidden)


def early_kernel(at, *refs):
    s_refs, w_refs = refs[:7], refs[7:15]
    k_ref, v_ref, gain_ref, out_ref, s_buf, w_buf, k_buf, v_buf, s_sem, w_sem, kv_sem = refs[15:]
    k_copy = pltpu.make_async_copy(k_ref.at[:, :, at[0]], k_buf, kv_sem.at[0])
    v_copy = pltpu.make_async_copy(v_ref.at[:, :, at[0]], v_buf, kv_sem.at[1])
    s_copies, w_copies = [], []
    for index, ref in enumerate(s_refs):
        for half in range(2):
            source = ref.at[:, pl.ds(528 * half, 512)]
            target = s_buf.at[at[6 + index], :, pl.ds(512 * half, 512)]
            s_copies.append(pltpu.make_async_copy(source, target, s_sem.at[2 * index + half]))
    for group in range(3):
        for step in range(4):
            ref = w_refs[(0, 4, 4)[group] + step]
            rows = ref.at[pl.ds(256 if group == 2 else 0, 256)]
            target = w_buf.at[group, at[14 + step]]
            w_copies.append(pltpu.make_async_copy(rows, target, w_sem.at[4 * group + step]))
    for copy in s_copies + w_copies[:4] + [k_copy, v_copy] + w_copies[4:]:
        copy.start()
    for copy in s_copies:
        copy.wait()
    for group in range(3):
        for step in range(4):
            w_copies[4 * group + step].wait()
        if group == 0:
            k_copy.wait()
            v_copy.wait()
        place = at[2 + group]

        def add(first, count):
            for half in range(2):
                rows = pl.ds(512 * half, 512)
                wide, narrow = block_product(
                    s_buf, w_buf.at[group], k_buf, v_buf, gain_ref, place, first, count, rows
                )
                if group == 0:
                    out_ref[rows, :WIDTH] = wide
                    out_ref[rows, WIDTH:] = narrow
                else:
                    out_ref[rows, :WIDTH] += wide
                    out_ref[rows, WIDTH:] += narrow

        @pl.when(2 * place + 1 - at[18] != at[13])
        def _():
            add(0, 2)

        @pl.when(2 * place + 1 - at[18] == at[13])
        def _():
            add(at[18], 1)


def block_product(s_buf, w_ref, k_buf, v_buf, gain_ref, place, first, count, rows):
    parts = []
    for step in range(count):
        slot = 2 * place + first + step
        for part in range(2):
            block = s_buf[slot, part, rows, :].astype(F32)
            parts.append((block * gain_ref[pl.ds(2 * slot + part, 1), :]).astype(BF))
    s = jnp.concatenate(parts, axis=1)
    blocks = pl.ds(2 * first, 2 * count)
    depth = 512 * count
    kv = jnp.concatenate(
        [ref[place, blocks].reshape(depth, HS) for ref in (k_buf, v_buf)], axis=1
    )
    wide = jnp.dot(s, w_ref[blocks].reshape(depth, WIDTH), preferred_element_type=F32)
    return wide, jnp.dot(s, kv, preferred_element_type=F32)


def final_kernel(half, at, *refs):
    s_refs, w_refs = refs[:8], refs[8:20]
    k_ref, v_ref, gain_ref, early_ref, out_ref, lead_ref, scale_ref = refs[20:27]
    s_buf, w_buf, k_buf, v_buf, sq_buf, lead_buf, acc, s_sem, w_sem, kv_sem, sq_sem = refs[27:]
    total = acc if half else out_ref
    last, place = at[13], at[5]
    copies = []
    for index, ref in enumerate(s_refs):
        rows = ref.at[0, pl.ds(528 * half + 512, 16)]
        copy = pltpu.make_async_copy(rows, sq_buf.at[index], sq_sem.at[index])
        copy.start()
        copies.append(copy)
    k_copy = pltpu.make_async_copy(k_ref.at[:, :, at[0]], k_buf, kv_sem.at[0])
    v_copy = pltpu.make_async_copy(v_ref.at[:, :, at[0]], v_buf, kv_sem.at[1])
    k_copy.start()
    v_copy.start()
    wanted = []
    for index, ref in enumerate(s_refs):
        slot = at[6 + index]
        rows = ref.at[:, pl.ds(528 * half, 512)]
        copy = pltpu.make_async_copy(rows, s_buf.at[slot], s_sem.at[index])
        wanted.append(((slot // 2 == place) | (slot == last), copy))
        rows = ref.at[0, pl.ds(528 * half, 512)]
        copy = pltpu.make_async_copy(rows, lead_buf, sq_sem.at[8 + index])
        wanted.append((slot == 0, copy))
    for step in range(4):
        target = w_buf.at[1, at[14 + step]]
        copy = pltpu.make_async_copy(w_refs[8 + step], target, w_sem.at[12 + step])
        wanted.append((at[0] >= 0, copy))
        for group in range(3):
            ref = w_refs[(0, 4, 4)[group] + step]
            rows = ref.at[pl.ds(256 if group == 2 else 0, 256)]
            target = w_buf.at[0, at[14 + step]]
            copy = pltpu.make_async_copy(rows, target, w_sem.at[4 * group + step])
            wanted.append((2 * at[2 + group] + 1 - at[18] == last, copy))
    for needed, copy in wanted:
        pl.when(needed)(copy.start)

    for copy in copies:
        copy.wait()
    squares = jnp.zeros((16, 256), F32)
    for index in range(8):
        squares += sq_buf[index].astype(F32)
    scales = []
    for stream in range(2):
        square = squares[3 * stream : 3 * stream + 1]
        square += squares[3 * stream + 1 : 3 * stream + 2] + squares[3 * stream + 2 : 3 * stream + 3]
        scale = lax.rsqrt(square / 8192.0 + EPS)
        scales.append(jnp.broadcast_to(scale, (128, 256)).T)
    scale = jnp.concatenate(scales, axis=0)
    scale_ref[...] = scale
    k_copy.wait()
    v_copy.wait()
    for needed, copy in wanted:
        pl.when(needed)(copy.wait)
    lead = lead_buf[...].astype(F32) * jnp.concatenate([scale, scale], axis=1)
    lead_ref[...] = (lead * gain_ref[pl.ds(0, 1), :]).astype(BF)

    everything = pl.ds(0, 512)
    wide, narrow = block_product(
        s_buf, w_buf.at[1], k_buf, v_buf, gain_ref, place, 0, 2, everything
    )
    total[:, :WIDTH] = wide + early_ref[:, :WIDTH]
    total[:, WIDTH:] = narrow + early_ref[:, WIDTH:]

    @pl.when(last // 2 != place)
    def _():
        wide, narrow = block_product(
            s_buf, w_buf.at[0], k_buf, v_buf, gain_ref, last // 2, 1 - at[18], 1, everything
        )
        total[:, :WIDTH] += wide
        total[:, WIDTH:] += narrow

    if half:
        out_ref[...] = acc[...].astype(BF)


def apart(value):
    return pltpu.with_memory_space_constraint(value, pltpu.HBM)


def whole(*shape):
    return pl.BlockSpec(shape, lambda i, at: (0,) * len(shape))


def project_early(at, pieces, rows, w_key, w_value, gain):
    return pl.pallas_call(
        early_kernel,
        grid_spec=pltpu.PrefetchScalarGridSpec(
            num_scalar_prefetch=1,
            grid=(1,),
            in_specs=[pl.BlockSpec(memory_space=pltpu.HBM)] * 17 + [whole(16, 256)],
            out_specs=whole(1024, 1280),
            scratch_shapes=[
                pltpu.VMEM((8, 2, 1024, 256), BF),
                pltpu.VMEM((3, 4, 256, WIDTH), BF),
                pltpu.VMEM((4, 4, 256, HS), BF),
                pltpu.VMEM((4, 4, 256, HS), BF),
                pltpu.SemaphoreType.DMA((14,)),
                pltpu.SemaphoreType.DMA((12,)),
                pltpu.SemaphoreType.DMA((2,)),
            ],
        ),
        out_shape=jax.ShapeDtypeStruct((1024, 1280), F32),
        compiler_params=params(40),
        cost_estimate=cost(2 * 1024 * 3072 * 1280, 24 * 2**20),
    )(at, *map(apart, pieces), *map(apart, rows), apart(w_key), apart(w_value), gain)


def project(half, at, pieces, rows, w_key, w_value, gain, early):
    return pl.pallas_call(
        functools.partial(final_kernel, half),
        grid_spec=pltpu.PrefetchScalarGridSpec(
            num_scalar_prefetch=1,
            grid=(1,),
            in_specs=[pl.BlockSpec(memory_space=pltpu.HBM)] * 22
            + [whole(16, 256), pl.BlockSpec((512, 1280), lambda i, at: (half, 0))],
            out_specs=[whole(512, 1280), whole(512, 256), whole(512, 128)],
            scratch_shapes=[
                pltpu.VMEM((8, 2, 512, 256), BF),
                pltpu.VMEM((2, 4, 256, WIDTH), BF),
                pltpu.VMEM((4, 4, 256, HS), BF),
                pltpu.VMEM((4, 4, 256, HS), BF),
                pltpu.VMEM((8, 16, 256), BF),
                pltpu.VMEM((512, 256), BF),
                pltpu.VMEM((512, 1280) if half else (8, 128), F32),
                pltpu.SemaphoreType.DMA((8,)),
                pltpu.SemaphoreType.DMA((16,)),
                pltpu.SemaphoreType.DMA((2,)),
                pltpu.SemaphoreType.DMA((16,)),
            ],
        ),
        out_shape=[
            jax.ShapeDtypeStruct((512, 1280), BF if half else F32),
            jax.ShapeDtypeStruct((512, 256), BF),
            jax.ShapeDtypeStruct((512, 128), F32),
        ],
        compiler_params=params(40),
        cost_estimate=cost(2 * 512 * 1280 * 1280, 12 * 2**20),
    )(at, *map(apart, pieces), *map(apart, rows), apart(w_key), apart(w_value), gain, early)


def rope_tables():
    half = HS // 2
    frequency = ROPE_BASE ** (-jnp.arange(half, dtype=F32) * 2.0 / HS)
    angles = jnp.arange(LEN, dtype=F32)[:, None] * frequency[None, :]
    cosine, sine = jnp.cos(angles), jnp.sin(angles)
    return jnp.concatenate([cosine, cosine], 1), jnp.concatenate([-sine, sine], 1)


def attended_columns(own_ref, got_ref, scale_ref, col_ref, row_ref, cos_ref, sin_ref):
    cosine, sine = cos_ref[...], sin_ref[...]

    def columns(at):
        cols = pl.ds(at * HS, HS)
        total = own_ref[0, 0, :, cols] + got_ref[0, 0, :, cols].astype(F32)
        return total * scale_ref[0, 0]

    def rotate(block):
        return (block * cosine + pltpu.roll(block, HS // 2, 1) * sine).astype(BF)

    keys = rotate(columns(QH))
    values = columns(QH + 1).astype(BF)
    row = lax.broadcasted_iota(jnp.int32, (LEN, LEN), 0)
    col = lax.broadcasted_iota(jnp.int32, (LEN, LEN), 1)
    allowed = (col_ref[0] == row_ref[0]) & (col <= row)
    nt = (((1,), (1,)), ((), ()))
    queries = jnp.concatenate([rotate(columns(head)) for head in range(QH)], axis=0)
    scores = lax.dot_general(queries, keys, nt, preferred_element_type=F32) * HS ** (-0.5)
    scores = jnp.where(jnp.concatenate([allowed] * QH, axis=0), scores, -1e30)
    exponent = jnp.exp(scores - jnp.max(scores, axis=-1, keepdims=True))
    weights = (exponent / jnp.sum(exponent, axis=-1, keepdims=True)).astype(BF)
    attended = lax.dot_general(
        values, weights, (((0,), (1,)), ((), ())), preferred_element_type=F32
    ).astype(BF)
    return [attended[:, head * LEN : (head + 1) * LEN] for head in range(QH)]


def attend_kernel(own_ref, got_ref, scale_ref, col_ref, row_ref, cos_ref, sin_ref, out_ref):
    blocks = attended_columns(own_ref, got_ref, scale_ref, col_ref, row_ref, cos_ref, sin_ref)
    for head, block in enumerate(blocks):
        out_ref[pl.ds(head * HS, HS), :] = block


def attend_diff_kernel(
    core, own_ref, got_ref, scale_ref, col_ref, row_ref, cos_ref, sin_ref, q_ref, keep_ref, give_ref
):
    blocks = attended_columns(own_ref, got_ref, scale_ref, col_ref, row_ref, cos_ref, sin_ref)
    first = core[0] == 0
    for head, block in enumerate(blocks):
        diff = block.astype(F32) - q_ref[pl.ds(head * HS, HS), :].astype(F32)
        diff = diff.reshape(2, 2, 32, LEN)
        keep_ref[pl.ds(head * 2, 2)] = jnp.where(first, diff[:, 0], diff[:, 1]).astype(BF)
        give_ref[pl.ds(head * 2, 2)] = jnp.where(first, diff[:, 1], diff[:, 0]).astype(BF)


def attend(own_rows, got_rows, scale, ids, tables):
    rows = pl.BlockSpec((1, 1, LEN, 1280), lambda s: (0, s, 0, 0))
    scales = pl.BlockSpec((1, 1, LEN, HS), lambda s: (0, s, 0, 0))
    table = pl.BlockSpec((LEN, HS), lambda s: (0, 0))
    return pl.pallas_call(
        attend_kernel,
        grid=(2,),
        in_specs=[
            rows,
            rows,
            scales,
            pl.BlockSpec((1, LEN, 1), lambda s: (s, 0, 0)),
            pl.BlockSpec((1, 1, LEN), lambda s: (s, 0, 0)),
            table,
            table,
        ],
        out_specs=pl.BlockSpec((WIDTH, LEN), lambda s: (0, s)),
        out_shape=jax.ShapeDtypeStruct((WIDTH, 256), BF),
        compiler_params=params(16),
        cost_estimate=cost(2**27, 2**21),
    )(own_rows, got_rows, scale, ids[:, :, None], ids[:, None, :], *tables)


def attend_diff(core, own_rows, got_rows, scale, ids, tables, att_q):
    rows = pl.BlockSpec((1, 1, LEN, 1280), lambda s, c: (1, s, 0, 0))
    scales = pl.BlockSpec((1, 1, LEN, HS), lambda s, c: (1, s, 0, 0))
    table = pl.BlockSpec((LEN, HS), lambda s, c: (0, 0))
    half = pl.BlockSpec((16, 32, LEN), lambda s, c: (0, 0, s))
    return pl.pallas_call(
        attend_diff_kernel,
        grid_spec=pltpu.PrefetchScalarGridSpec(
            num_scalar_prefetch=1,
            grid=(2,),
            in_specs=[
                rows,
                rows,
                scales,
                pl.BlockSpec((1, LEN, 1), lambda s, c: (s, 0, 0)),
                pl.BlockSpec((1, 1, LEN), lambda s, c: (s, 0, 0)),
                table,
                table,
                pl.BlockSpec((WIDTH, LEN), lambda s, c: (0, s)),
            ],
            out_specs=[half, half],
        ),
        out_shape=[jax.ShapeDtypeStruct((16, 32, 256), BF)] * 2,
        compiler_params=params(16),
        cost_estimate=cost(2**27, 2**21),
    )(core, own_rows, got_rows, scale, ids[:, :, None], ids[:, None, :], *tables, att_q)


def moments_kernel(axis, place, left_ref, left_sib_ref, right_ref, right_sib_ref, *refs):
    nt = (((1,), (1,)), ((), ()))
    out_ref = refs[-1]

    def rows(ref):
        parts = []
        for step in range(4):
            near = (place[1 + axis] + step) % 4
            part = ref[:, near, 0] if axis else ref[near, :, 0]
            parts.append(part.reshape(128, 256))
        return jnp.concatenate(parts, axis=0)

    total = lax.dot_general(rows(left_ref), right_ref[...], nt, preferred_element_type=F32)
    total += lax.dot_general(
        rows(left_sib_ref), right_sib_ref[...], nt, preferred_element_type=F32
    )
    out_ref[:, :, :32] = total.astype(BF).reshape(4, 4, 32, WIDTH)
    if len(refs) == 2:
        for step in range(4):
            out_ref[step, :, 32:] = refs[0][:, (place[2] + step) % 4]


def moments(axis, place, left, left_sib, right, right_sib, *more):
    def side(value):
        if value.shape[0] == 16:
            value = value.reshape(4, 4, 1, 32, 256)
            return value, pl.BlockSpec((4, 4, 1, 32, 256), lambda i, p: (0, 0, 0, 0, 0))
        value = value.reshape(4, 4, 2, 32, 256)
        return value, pl.BlockSpec((4, 4, 1, 32, 256), lambda i, p: (0, 0, p[0], 0, 0))

    left, left_spec = side(left)
    left_sib, left_sib_spec = side(left_sib)
    whole = pl.BlockSpec((WIDTH, 256), lambda i, p: (0, 0))
    rows = 48 if more else 32
    return pl.pallas_call(
        functools.partial(moments_kernel, axis),
        grid_spec=pltpu.PrefetchScalarGridSpec(
            num_scalar_prefetch=1,
            grid=(1,),
            in_specs=[left_spec, left_sib_spec, whole, whole]
            + [pl.BlockSpec((4, 4, 16, WIDTH), lambda i, p: (0, 0, 0, 0))] * len(more),
            out_specs=pl.BlockSpec((4, 4, rows, WIDTH), lambda i, p: (0, 0, 0, 0)),
        ),
        out_shape=jax.ShapeDtypeStruct((4, 4, rows, WIDTH), BF),
        compiler_params=params(24),
        cost_estimate=cost(2**30, 2**21),
    )(place, left, left_sib, right, right_sib, *more)


def band_kernel(
    place, gain_ref, own_ref, sib_ref, got_own_ref, got_sib_ref, scale_ref, scale_sib_ref, piece_ref, out_ref
):
    first = place[0] == 0
    tn = (((0,), (0,)), ((), ()))
    for part in range(2):
        gram = jnp.zeros((256, 256), F32)
        delta = jnp.zeros((256, 256), F32)
        for half, (mine, got, scales) in enumerate(
            ((own_ref, got_sib_ref, scale_ref), (sib_ref, got_own_ref, scale_sib_ref))
        ):
            lead = jnp.where(first, mine[...], got[...])
            lead_q, lead_f = lead[:256], lead[256:]
            diff = (lead_f.astype(F32) - lead_q.astype(F32)).astype(BF)
            scale = scales[:256, :]
            right = piece_ref[part, pl.ds(528 * half, 256)].astype(F32)
            right = right * jnp.concatenate([scale, scale], axis=1)
            right = (right * gain_ref[pl.ds(2 * place[3] + part, 1), :]).astype(BF)
            gram += lax.dot_general(lead_q, right, tn, preferred_element_type=F32)
            delta += lax.dot_general(diff, right, tn, preferred_element_type=F32)
        for index, value in enumerate((gram, delta)):
            cols = pl.ds(index * 512 + part * 256, 256)
            out_ref[:, :, :, cols] = value.astype(BF).reshape(4, 4, 16, 256)


def band_moments(place, *sides):
    return pl.pallas_call(
        band_kernel,
        in_specs=[pl.BlockSpec(memory_space=pltpu.SMEM)]
        + [pl.BlockSpec(memory_space=pltpu.VMEM)] * len(sides),
        out_specs=pl.BlockSpec(memory_space=pltpu.VMEM),
        out_shape=jax.ShapeDtypeStruct((4, 4, 16, WIDTH), BF),
        compiler_params=params(16),
        cost_estimate=cost(2**29, 2**21),
    )(place, *sides)


def scatter(parts, axis, here):
    total = take(parts, here, 0).astype(F32)
    for step in (1, 3, 2):
        total = total + shift(take(parts, (here + step) % 4, 0), axis, step).astype(F32)
    return total


MOVES = {
    "zA": ("w", "zh", 1),
    "zB": ("w", "zh", -1),
    "zF": ("zA", "zh", 1),
    "l": ("p", "zl", 1),
}
for block, axis in (("w", "y"), ("pair", "y"), ("zF", "y"), ("p", "x"), ("l", "x")):
    MOVES[block + ".A"] = (block, axis, 1)
    MOVES[block + ".B"] = (block, axis, -1)
    MOVES[block + ".F"] = (block + ".A", axis, 1)
MOVES["zF.F"] = ("zF", "y", 2)
STEPS = (
    ("zA", "w.A", "p.A"),
    ("zB", "w.B"),
    ("w.F", "p.B", "l"),
    ("pair.A", "p.F"),
    ("pair.B", "l.A", "zF"),
    ("pair.F", "l.B"),
    ("zF.A", "zF.B", "l.F"),
    ("zF.F",),
)


def gate(*values):
    return pl.pallas_call(
        lambda *refs: None,
        in_specs=[pl.BlockSpec(memory_space=pl.ANY)] * len(values),
        out_specs=[pl.BlockSpec(memory_space=pl.ANY)] * len(values),
        out_shape=[jax.ShapeDtypeStruct(v.shape, v.dtype) for v in values],
        input_output_aliases={i: i for i in range(len(values))},
        cost_estimate=cost(2**34, 2**25),
    )(*values)


def exchange(env):
    order = jnp.zeros((8, 128), F32)
    for index, starts in enumerate(STEPS):
        if index >= 2:
            held = set(STEPS[index - 2]) | {MOVES[name][0] for name in starts} - {"w"}
            if index == 3:
                env["pair"] = jnp.concatenate([env["zA"], env["zB"]])
            held = sorted(held)
            *values, order = gate(*(env[name] for name in held), order)
            env.update(zip(held, values))
        for name in starts:
            source, axis, step = MOVES[name]
            env[name] = (shift if axis == "zl" else turn)(env[source], axis, step)
    return env


def local(hidden, hidden_q, norm_gain, doc_ids, w_query, w_key, w_value):
    dp, tensor = lax.axis_index("dp"), lax.axis_index("tensor")
    zh, y, c = dp // 8, dp // 2 % 4, dp % 2
    x, zl = tensor // 2, tensor % 2
    sign = 1 - 2 * c

    keep, give = prepare(c.reshape(1), hidden_q, hidden)
    piece = jnp.concatenate([keep, shift(give, "c", 1)], 1)
    env = exchange({"w": w_query, "p": piece})

    gain = take(norm_gain.reshape(16, 2, 256), c, 1)
    steps = (("", 0), (".A", -sign), (".B", sign), (".F", 2))
    at = [c, tensor] + [(zh + dz) % 4 for _, dz in steps]
    for block, dz in (("p", 0), ("l", 1)):
        at += [(x + dx) % 4 * 2 + (zl + dz) % 2 for _, dx in steps]
    at = jnp.stack(at + [(y + dy) % 4 for _, dy in steps] + [zl])
    rows = [env[block + name] for block in ("w", "pair", "zF") for name, _ in steps]
    pieces = [env[block + name] for block in ("p", "l") for name, _ in steps]

    w_key = w_key.reshape(4, 4, 2, 256, HS)
    w_value = w_value.reshape(4, 4, 2, 256, HS)
    early = project_early(at, pieces[:7], rows[:8], w_key, w_value, gain)
    sib_rows, lead_sib, scale_sib = project(1, at, pieces, rows, w_key, w_value, gain, early)
    got_rows = shift(sib_rows, "c", 1).reshape(2, 2, LEN, 1280)
    got_lead = shift(lead_sib, "c", 1)
    own_rows, lead, scale = project(0, at, pieces, rows, w_key, w_value, gain, early)
    own_rows = own_rows.reshape(2, 2, LEN, 1280)
    scales = scale.reshape(2, 2, LEN, HS)
    got_lead_sib = shift(lead, "c", 1)
    tables = rope_tables()
    place = jnp.stack([c, zh, y, tensor])
    att_q = attend(own_rows, got_rows, scales, doc_ids, tables)
    att_sib = shift(att_q, "c", 1)
    lead, att_q = lax.optimization_barrier((lead, att_q))
    band = band_moments(
        place, gain, lead, lead_sib, got_lead_sib, got_lead, scale, scale_sib, env["p"]
    )
    keep, give = attend_diff(c.reshape(1), own_rows, got_rows, scales, doc_ids, tables, att_q)
    keep_sib = shift(give, "c", 1)
    here = {"zh": zh, "y": y}
    outs = []
    for left, left_sib, axis, other, more in (
        (keep, keep_sib, "zh", "y", ()),
        (att_q, att_sib, "y", "zh", (band,)),
    ):
        sums = moments(int(axis == "y"), place, left, left_sib, att_q, att_sib, *more)
        total = sums[0].astype(F32)
        for step in (2, 1, 3):
            total = total + shift(sums[step], axis, step).astype(F32)
        outs.append(scatter(total.astype(BF), other, here[other]) / TOKENS)
    head_delta, head_gram = outs

    band = head_gram[32:].reshape(2, 8, 2, 2, 256).transpose(2, 0, 1, 3, 4)
    other = shift(take(band, 1 - c, 1), "c", 1)
    mine = take(band, c, 1)
    band = jnp.stack(
        [jnp.where(c == 0, mine, other), jnp.where(c == 0, other, mine)], 3
    ).reshape(2, 8, WIDTH)
    return band[0], band[1], head_gram[None, :32], head_delta[None]


def solution(mesh):
    return jax.shard_map(
        local,
        mesh=mesh,
        in_specs=(
            P("dp", "tensor"),
            P("dp", "tensor"),
            P(),
            P("dp", None),
            P("dp", "tensor"),
            P(None, "tensor"),
            P(None, "tensor"),
        ),
        out_specs=(
            P("dp", "tensor"),
            P("dp", "tensor"),
            P("tensor", "dp", None),
            P("tensor", "dp", None),
        ),
        check_vma=False,
    )
```

```python
import functools

import functools

import jax
import jax.numpy as jnp
from jax import lax
from jax.experimental import pallas as pl
from jax.experimental.pallas import tpu as pltpu
from jax.sharding import PartitionSpec as P

HS = 128
QH = 8
LEN = 128
BAND = 256
WIDTH = 1024
TOKENS = 8192
EPS = 1e-05
ROPE_BASE = 500000.0
BF = jnp.bfloat16
F32 = jnp.float32

SIZES = {"zh": 4, "y": 4, "c": 2, "x": 4, "zl": 2}
STRIDES = {"zh": 64, "y": 16, "c": 8, "x": 2, "zl": 1}


def shift(value, axis, step):
    size, stride = SIZES[axis], STRIDES[axis]
    pairs = []
    for index in range(256):
        at = index // stride % size
        pairs.append((index, index + ((at + step) % size - at) * stride))
    return lax.ppermute(value, ("dp", "tensor"), pairs)


def turn(value, axis, step):
    size, stride = SIZES[axis], STRIDES[axis]
    pairs = []
    for index in range(256):
        at = index // stride % size
        own = -step if index // STRIDES["c"] % 2 else step
        pairs.append((index, index + ((at + own) % size - at) * stride))
    return lax.ppermute(value, ("dp", "tensor"), pairs)


def take(value, index, axis):
    return lax.dynamic_index_in_dim(value, index, axis, keepdims=False)


def params(mib):
    return pltpu.CompilerParams(vmem_limit_bytes=mib * 2**20)


def cost(flops, moved):
    return pl.CostEstimate(flops=flops, bytes_accessed=moved, transcendentals=0)


def prepare_kernel(core, q_ref, f_ref, keep_ref, give_ref):
    first = core[0] == 0
    ones = jnp.ones((8, WIDTH), BF)
    nt = (((1,), (1,)), ((), ()))
    terms = []
    for stream, ref in enumerate((q_ref, f_ref)):
        square = jnp.square(ref[...].astype(F32))
        high = square.astype(BF)
        low = (square - high.astype(F32)).astype(BF)
        total = lax.dot_general(ones, high, nt, preferred_element_type=F32)
        total += lax.dot_general(ones, low, nt, preferred_element_type=F32)
        for _ in range(3):
            term = total[:1].astype(BF).astype(F32)
            terms.append(term)
            total = total - term
        for part in range(2):
            even, odd = (ref[:, pl.ds(512 * part + 256 * k, 256)] for k in range(2))
            rows = pl.ds(256 * stream, 256)
            keep_ref[part, rows] = jnp.where(first, even, odd)
            give_ref[part, rows] = jnp.where(first, odd, even)
    extra = jnp.concatenate(terms + [jnp.zeros((10, 256), F32)], axis=0).astype(BF)
    for part in range(2):
        keep_ref[part, pl.ds(512, 16)] = extra
        give_ref[part, pl.ds(512, 16)] = extra


def prepare(core, hidden_q, hidden):
    return pl.pallas_call(
        prepare_kernel,
        in_specs=[pl.BlockSpec(memory_space=pltpu.SMEM)]
        + [pl.BlockSpec(memory_space=pltpu.VMEM)] * 2,
        out_specs=[pl.BlockSpec(memory_space=pltpu.VMEM)] * 2,
        out_shape=[jax.ShapeDtypeStruct((2, 528, 256), BF)] * 2,
        compiler_params=params(16),
        cost_estimate=cost(0, 2**21),
    )(core, hidden_q, hidden)


def early_kernel(at, *refs):
    s_refs, w_refs = refs[:7], refs[7:15]
    k_ref, v_ref, gain_ref, _, sums_ref, s_buf, w_buf, k_buf, v_buf, out_ref, s_sem, w_sem, kv_sem = refs[15:]
    k_copy = pltpu.make_async_copy(k_ref.at[:, :, at[0]], k_buf, kv_sem.at[0])
    v_copy = pltpu.make_async_copy(v_ref.at[:, :, at[0]], v_buf, kv_sem.at[1])
    s_copies, w_copies = [], []
    for index, ref in enumerate(s_refs):
        for half in range(2):
            source = ref.at[:, pl.ds(528 * half, 512)]
            target = s_buf.at[at[6 + index], :, pl.ds(512 * half, 512)]
            s_copies.append(pltpu.make_async_copy(source, target, s_sem.at[2 * index + half]))
    for group in range(3):
        for step in range(4):
            ref = w_refs[(0, 4, 4)[group] + step]
            rows = ref.at[pl.ds(256 if group == 2 else 0, 256)]
            target = w_buf.at[group, at[14 + step]]
            w_copies.append(pltpu.make_async_copy(rows, target, w_sem.at[4 * group + step]))
    for copy in s_copies + w_copies[:4] + [k_copy, v_copy] + w_copies[4:]:
        copy.start()
    for copy in s_copies:
        copy.wait()
    for group in range(3):
        for step in range(4):
            w_copies[4 * group + step].wait()
        if group == 0:
            k_copy.wait()
            v_copy.wait()
        place = at[2 + group]

        def add(first, count):
            rows = pl.ds(0, 1024)
            wide, narrow = block_product(
                s_buf, w_buf.at[group], k_buf, v_buf, gain_ref, place, first, count, rows
            )
            if group == 0:
                out_ref[:, :WIDTH] = wide
                out_ref[:, WIDTH:] = narrow
            else:
                out_ref[:, :WIDTH] += wide
                out_ref[:, WIDTH:] += narrow

        @pl.when(2 * place + 1 - at[18] != at[13])
        def _():
            add(0, 2)

        @pl.when(2 * place + 1 - at[18] == at[13])
        def _():
            add(at[18], 1)

    copy = pltpu.make_async_copy(out_ref, sums_ref, kv_sem.at[2])
    copy.start()
    copy.wait()


def block_product(s_buf, w_ref, k_buf, v_buf, gain_ref, place, first, count, rows):
    parts = []
    for step in range(count):
        slot = 2 * place + first + step
        for part in range(2):
            block = s_buf[slot, part, rows, :].astype(F32)
            parts.append((block * gain_ref[pl.ds(2 * slot + part, 1), :]).astype(BF))
    s = jnp.concatenate(parts, axis=1)
    blocks = pl.ds(2 * first, 2 * count)
    depth = 512 * count
    kv = jnp.concatenate(
        [ref[place, blocks].reshape(depth, HS) for ref in (k_buf, v_buf)], axis=1
    )
    wide = jnp.dot(s, w_ref[blocks].reshape(depth, WIDTH), preferred_element_type=F32)
    return wide, jnp.dot(s, kv, preferred_element_type=F32)


def final_kernel(at, *refs):
    s_refs, w_refs = refs[:8], refs[8:20]
    k_ref, v_ref, gain_ref, early_ref, out_ref, sib_ref, lead_ref, scale_ref = refs[20:28]
    s_buf, w_buf, k_buf, v_buf, sq_buf, lead_buf, acc, s_sem, w_sem, kv_sem, sq_sem = refs[28:]
    last, place = at[13], at[5]
    copies = []
    for index, ref in enumerate(s_refs):
        for half in range(2):
            rows = ref.at[0, pl.ds(528 * half + 512, 16)]
            target = sq_buf.at[half, index]
            copies.append(pltpu.make_async_copy(rows, target, sq_sem.at[2 * index + half]))
            copies[-1].start()
    k_copy = pltpu.make_async_copy(k_ref.at[:, :, at[0]], k_buf, kv_sem.at[0])
    v_copy = pltpu.make_async_copy(v_ref.at[:, :, at[0]], v_buf, kv_sem.at[1])
    early_copy = pltpu.make_async_copy(early_ref, acc, kv_sem.at[2])
    k_copy.start()
    v_copy.start()
    wanted = []
    for index, ref in enumerate(s_refs):
        slot = at[6 + index]
        for half in range(2):
            rows, target = pl.ds(528 * half, 512), pl.ds(512 * half, 512)
            sem = 2 * index + half
            copy = pltpu.make_async_copy(ref.at[:, rows], s_buf.at[slot, :, target], s_sem.at[sem])
            wanted.append(((slot // 2 == place) | (slot == last), copy))
            copy = pltpu.make_async_copy(ref.at[0, rows], lead_buf.at[target], sq_sem.at[16 + sem])
            wanted.append((slot == 0, copy))
    for step in range(4):
        target = w_buf.at[1, at[14 + step]]
        copy = pltpu.make_async_copy(w_refs[8 + step], target, w_sem.at[12 + step])
        wanted.append((at[0] >= 0, copy))
        for group in range(3):
            ref = w_refs[(0, 4, 4)[group] + step]
            rows = ref.at[pl.ds(256 if group == 2 else 0, 256)]
            target = w_buf.at[0, at[14 + step]]
            copy = pltpu.make_async_copy(rows, target, w_sem.at[4 * group + step])
            wanted.append((2 * at[2 + group] + 1 - at[18] == last, copy))
    for needed, copy in wanted:
        pl.when(needed)(copy.start)
    early_copy.start()

    for copy in copies:
        copy.wait()
    scales = []
    for half in range(2):
        squares = jnp.zeros((16, 256), F32)
        for index in range(8):
            squares += sq_buf[half, index].astype(F32)
        for first in (0, 3):
            square = squares[first : first + 1] + squares[first + 1 : first + 2]
            scale = lax.rsqrt((square + squares[first + 2 : first + 3]) / 8192.0 + EPS)
            scales.append(jnp.broadcast_to(scale, (128, 256)).T)
    scale = jnp.concatenate(scales, axis=0)
    scale_ref[...] = scale
    k_copy.wait()
    v_copy.wait()
    for needed, copy in wanted:
        pl.when(needed)(copy.wait)
    lead = lead_buf[...].astype(F32) * jnp.concatenate([scale, scale], axis=1)
    lead_ref[...] = (lead * gain_ref[pl.ds(0, 1), :]).astype(BF)

    everything = pl.ds(0, 1024)
    wide, narrow = block_product(
        s_buf, w_buf.at[1], k_buf, v_buf, gain_ref, place, 0, 2, everything
    )
    early_copy.wait()
    acc[:, :WIDTH] += wide
    acc[:, WIDTH:] += narrow

    @pl.when(last // 2 != place)
    def _():
        wide, narrow = block_product(
            s_buf, w_buf.at[0], k_buf, v_buf, gain_ref, last // 2, 1 - at[18], 1, everything
        )
        acc[:, :WIDTH] += wide
        acc[:, WIDTH:] += narrow

    out_ref[...] = acc[:512]
    sib_ref[...] = acc[512:].astype(BF)


def apart(value):
    return pltpu.with_memory_space_constraint(value, pltpu.HBM)


def whole(*shape):
    return pl.BlockSpec(shape, lambda i, at: (0,) * len(shape))


def project_early(at, pieces, rows, w_key, w_value, gain, room):
    return pl.pallas_call(
        early_kernel,
        grid_spec=pltpu.PrefetchScalarGridSpec(
            num_scalar_prefetch=1,
            grid=(1,),
            in_specs=[pl.BlockSpec(memory_space=pltpu.HBM)] * 17
            + [whole(16, 256), pl.BlockSpec(memory_space=pltpu.HBM)],
            out_specs=pl.BlockSpec(memory_space=pltpu.HBM),
            scratch_shapes=[
                pltpu.VMEM((8, 2, 1024, 256), BF),
                pltpu.VMEM((3, 4, 256, WIDTH), BF),
                pltpu.VMEM((4, 4, 256, HS), BF),
                pltpu.VMEM((4, 4, 256, HS), BF),
                pltpu.VMEM((1024, 1280), F32),
                pltpu.SemaphoreType.DMA((14,)),
                pltpu.SemaphoreType.DMA((12,)),
                pltpu.SemaphoreType.DMA((3,)),
            ],
        ),
        out_shape=jax.ShapeDtypeStruct((1024, 1280), F32),
        input_output_aliases={19: 0},
        compiler_params=params(40),
        cost_estimate=cost(2 * 1024 * 3072 * 1280, 24 * 2**20),
    )(at, *map(apart, pieces), *map(apart, rows), apart(w_key), apart(w_value), gain, apart(room))


def project(at, pieces, rows, w_key, w_value, gain, early):
    return pl.pallas_call(
        final_kernel,
        grid_spec=pltpu.PrefetchScalarGridSpec(
            num_scalar_prefetch=1,
            grid=(1,),
            in_specs=[pl.BlockSpec(memory_space=pltpu.HBM)] * 22
            + [whole(16, 256), pl.BlockSpec(memory_space=pl.ANY)],
            out_specs=[whole(512, 1280), whole(512, 1280), whole(1024, 256), whole(1024, 128)],
            scratch_shapes=[
                pltpu.VMEM((8, 2, 1024, 256), BF),
                pltpu.VMEM((2, 4, 256, WIDTH), BF),
                pltpu.VMEM((4, 4, 256, HS), BF),
                pltpu.VMEM((4, 4, 256, HS), BF),
                pltpu.VMEM((2, 8, 16, 256), BF),
                pltpu.VMEM((1024, 256), BF),
                pltpu.VMEM((1024, 1280), F32),
                pltpu.SemaphoreType.DMA((16,)),
                pltpu.SemaphoreType.DMA((16,)),
                pltpu.SemaphoreType.DMA((3,)),
                pltpu.SemaphoreType.DMA((32,)),
            ],
        ),
        out_shape=[
            jax.ShapeDtypeStruct((512, 1280), F32),
            jax.ShapeDtypeStruct((512, 1280), BF),
            jax.ShapeDtypeStruct((1024, 256), BF),
            jax.ShapeDtypeStruct((1024, 128), F32),
        ],
        compiler_params=params(36),
        cost_estimate=cost(2 * 1024 * 1280 * 1280, 20 * 2**20),
    )(at, *map(apart, pieces), *map(apart, rows), apart(w_key), apart(w_value), gain, apart(early))


def rope_tables():
    half = HS // 2
    frequency = ROPE_BASE ** (-jnp.arange(half, dtype=F32) * 2.0 / HS)
    angles = jnp.arange(LEN, dtype=F32)[:, None] * frequency[None, :]
    cosine, sine = jnp.cos(angles), jnp.sin(angles)
    return jnp.concatenate([cosine, cosine], 1), jnp.concatenate([-sine, sine], 1)


def attended_columns(own_ref, got_ref, scale_ref, col_ref, row_ref, cos_ref, sin_ref):
    cosine, sine = cos_ref[...], sin_ref[...]

    def columns(at):
        cols = pl.ds(at * HS, HS)
        total = own_ref[0, 0, :, cols] + got_ref[0, 0, :, cols].astype(F32)
        return total * scale_ref[0, 0]

    def rotate(block):
        return (block * cosine + pltpu.roll(block, HS // 2, 1) * sine).astype(BF)

    keys = rotate(columns(QH))
    values = columns(QH + 1).astype(BF)
    row = lax.broadcasted_iota(jnp.int32, (LEN, LEN), 0)
    col = lax.broadcasted_iota(jnp.int32, (LEN, LEN), 1)
    allowed = (col_ref[0] == row_ref[0]) & (col <= row)
    nt = (((1,), (1,)), ((), ()))
    queries = jnp.concatenate([rotate(columns(head)) for head in range(QH)], axis=0)
    scores = lax.dot_general(queries, keys, nt, preferred_element_type=F32) * HS ** (-0.5)
    scores = jnp.where(jnp.concatenate([allowed] * QH, axis=0), scores, -1e30)
    exponent = jnp.exp(scores - jnp.max(scores, axis=-1, keepdims=True))
    weights = (exponent / jnp.sum(exponent, axis=-1, keepdims=True)).astype(BF)
    attended = lax.dot_general(
        values, weights, (((0,), (1,)), ((), ())), preferred_element_type=F32
    ).astype(BF)
    return [attended[:, head * LEN : (head + 1) * LEN] for head in range(QH)]


def attend_kernel(own_ref, got_ref, scale_ref, col_ref, row_ref, cos_ref, sin_ref, out_ref):
    blocks = attended_columns(own_ref, got_ref, scale_ref, col_ref, row_ref, cos_ref, sin_ref)
    for head, block in enumerate(blocks):
        out_ref[pl.ds(head * HS, HS), :] = block


def attend_diff_kernel(
    core, own_ref, got_ref, scale_ref, col_ref, row_ref, cos_ref, sin_ref, q_ref, keep_ref, give_ref
):
    blocks = attended_columns(own_ref, got_ref, scale_ref, col_ref, row_ref, cos_ref, sin_ref)
    first = core[0] == 0
    for head, block in enumerate(blocks):
        diff = block.astype(F32) - q_ref[pl.ds(head * HS, HS), :].astype(F32)
        diff = diff.reshape(2, 2, 32, LEN)
        keep_ref[pl.ds(head * 2, 2)] = jnp.where(first, diff[:, 0], diff[:, 1]).astype(BF)
        give_ref[pl.ds(head * 2, 2)] = jnp.where(first, diff[:, 1], diff[:, 0]).astype(BF)


def attend(own_rows, got_rows, scale, ids, tables):
    rows = pl.BlockSpec((1, 1, LEN, 1280), lambda s: (0, s, 0, 0))
    scales = pl.BlockSpec((1, 1, LEN, HS), lambda s: (0, s, 0, 0))
    table = pl.BlockSpec((LEN, HS), lambda s: (0, 0))
    return pl.pallas_call(
        attend_kernel,
        grid=(2,),
        in_specs=[
            rows,
            rows,
            scales,
            pl.BlockSpec((1, LEN, 1), lambda s: (s, 0, 0)),
            pl.BlockSpec((1, 1, LEN), lambda s: (s, 0, 0)),
            table,
            table,
        ],
        out_specs=pl.BlockSpec((WIDTH, LEN), lambda s: (0, s)),
        out_shape=jax.ShapeDtypeStruct((WIDTH, 256), BF),
        compiler_params=params(16),
        cost_estimate=cost(2**27, 2**21),
    )(own_rows, got_rows, scale, ids[:, :, None], ids[:, None, :], *tables)


def attend_diff(core, own_rows, got_rows, scale, ids, tables, att_q):
    rows = pl.BlockSpec((1, 1, LEN, 1280), lambda s, c: (1, s, 0, 0))
    scales = pl.BlockSpec((1, 1, LEN, HS), lambda s, c: (1, s, 0, 0))
    table = pl.BlockSpec((LEN, HS), lambda s, c: (0, 0))
    half = pl.BlockSpec((16, 32, LEN), lambda s, c: (0, 0, s))
    return pl.pallas_call(
        attend_diff_kernel,
        grid_spec=pltpu.PrefetchScalarGridSpec(
            num_scalar_prefetch=1,
            grid=(2,),
            in_specs=[
                rows,
                rows,
                scales,
                pl.BlockSpec((1, LEN, 1), lambda s, c: (s, 0, 0)),
                pl.BlockSpec((1, 1, LEN), lambda s, c: (s, 0, 0)),
                table,
                table,
                pl.BlockSpec((WIDTH, LEN), lambda s, c: (0, s)),
            ],
            out_specs=[half, half],
        ),
        out_shape=[jax.ShapeDtypeStruct((16, 32, 256), BF)] * 2,
        compiler_params=params(16),
        cost_estimate=cost(2**27, 2**21),
    )(core, own_rows, got_rows, scale, ids[:, :, None], ids[:, None, :], *tables, att_q)


def moments_kernel(axis, place, left_ref, left_sib_ref, right_ref, right_sib_ref, *refs):
    nt = (((1,), (1,)), ((), ()))
    out_ref = refs[-1]

    def rows(ref):
        parts = []
        for step in range(4):
            near = (place[1 + axis] + step) % 4
            part = ref[:, near, 0] if axis else ref[near, :, 0]
            parts.append(part.reshape(128, 256))
        return jnp.concatenate(parts, axis=0)

    total = lax.dot_general(rows(left_ref), right_ref[...], nt, preferred_element_type=F32)
    total += lax.dot_general(
        rows(left_sib_ref), right_sib_ref[...], nt, preferred_element_type=F32
    )
    out_ref[:, :, :32] = total.astype(BF).reshape(4, 4, 32, WIDTH)
    if len(refs) == 2:
        for step in range(4):
            out_ref[step, :, 32:] = refs[0][:, (place[2] + step) % 4]


def moments(axis, place, left, left_sib, right, right_sib, *more):
    def side(value):
        if value.shape[0] == 16:
            value = value.reshape(4, 4, 1, 32, 256)
            return value, pl.BlockSpec((4, 4, 1, 32, 256), lambda i, p: (0, 0, 0, 0, 0))
        value = value.reshape(4, 4, 2, 32, 256)
        return value, pl.BlockSpec((4, 4, 1, 32, 256), lambda i, p: (0, 0, p[0], 0, 0))

    left, left_spec = side(left)
    left_sib, left_sib_spec = side(left_sib)
    whole = pl.BlockSpec((WIDTH, 256), lambda i, p: (0, 0))
    rows = 48 if more else 32
    return pl.pallas_call(
        functools.partial(moments_kernel, axis),
        grid_spec=pltpu.PrefetchScalarGridSpec(
            num_scalar_prefetch=1,
            grid=(1,),
            in_specs=[left_spec, left_sib_spec, whole, whole]
            + [pl.BlockSpec((4, 4, 16, WIDTH), lambda i, p: (0, 0, 0, 0))] * len(more),
            out_specs=pl.BlockSpec((4, 4, rows, WIDTH), lambda i, p: (0, 0, 0, 0)),
        ),
        out_shape=jax.ShapeDtypeStruct((4, 4, rows, WIDTH), BF),
        compiler_params=params(24),
        cost_estimate=cost(2**30, 2**21),
    )(place, left, left_sib, right, right_sib, *more)


def band_kernel(place, gain_ref, lead_ref, got_ref, scale_ref, piece_ref, out_ref):
    first = place[0] == 0
    tn = (((0,), (0,)), ((), ()))
    for part in range(2):
        gram = jnp.zeros((256, 256), F32)
        delta = jnp.zeros((256, 256), F32)
        for half in range(2):
            mine, theirs = pl.ds(512 * half, 512), pl.ds(512 - 512 * half, 512)
            lead = jnp.where(first, lead_ref[mine, :], got_ref[theirs, :])
            lead_q, lead_f = lead[:256], lead[256:]
            diff = (lead_f.astype(F32) - lead_q.astype(F32)).astype(BF)
            scale = scale_ref[pl.ds(512 * half, 256), :]
            right = piece_ref[part, pl.ds(528 * half, 256)].astype(F32)
            right = right * jnp.concatenate([scale, scale], axis=1)
            right = (right * gain_ref[pl.ds(2 * place[3] + part, 1), :]).astype(BF)
            gram += lax.dot_general(lead_q, right, tn, preferred_element_type=F32)
            delta += lax.dot_general(diff, right, tn, preferred_element_type=F32)
        for index, value in enumerate((gram, delta)):
            cols = pl.ds(index * 512 + part * 256, 256)
            out_ref[:, :, :, cols] = value.astype(BF).reshape(4, 4, 16, 256)


def band_moments(place, *sides):
    return pl.pallas_call(
        band_kernel,
        in_specs=[pl.BlockSpec(memory_space=pltpu.SMEM)]
        + [pl.BlockSpec(memory_space=pltpu.VMEM)] * len(sides),
        out_specs=pl.BlockSpec(memory_space=pltpu.VMEM),
        out_shape=jax.ShapeDtypeStruct((4, 4, 16, WIDTH), BF),
        compiler_params=params(16),
        cost_estimate=cost(2**29, 2**21),
    )(place, *sides)


def scatter(parts, axis, here):
    total = take(parts, here, 0).astype(F32)
    for step in (1, 3, 2):
        total = total + shift(take(parts, (here + step) % 4, 0), axis, step).astype(F32)
    return total


MOVES = {
    "zA": ("w", "zh", 1),
    "zB": ("w", "zh", -1),
    "zF": ("zA", "zh", 1),
    "l": ("p", "zl", 1),
}
for block, axis in (("w", "y"), ("pair", "y"), ("zF", "y"), ("p", "x"), ("l", "x")):
    MOVES[block + ".A"] = (block, axis, 1)
    MOVES[block + ".B"] = (block, axis, -1)
    MOVES[block + ".F"] = (block + ".A", axis, 1)
MOVES["zF.F"] = ("zF", "y", 2)
STEPS = (
    ((), ("zA", "zB", "w.A", "w.B", "p.A")),
    (("zA", "zB", "w.A", "w.B", "p.A"), ("l", "pair.A", "pair.B", "p.B", "p.F")),
    (("l", "pair.A", "pair.B", "p.B", "p.F"), ("pair.F", "zF", "l.A", "l.B", "w.F")),
    (("pair.F", "zF"), ("zF.A", "zF.B", "zF.F")),
    (("l.A", "l.B", "w.F"), ("l.F",)),
    (("zF.A", "zF.B", "zF.F"), ()),
)


def gate(*values):
    return pl.pallas_call(
        lambda *refs: None,
        in_specs=[pl.BlockSpec(memory_space=pl.ANY)] * len(values),
        out_specs=[pl.BlockSpec(memory_space=pl.ANY)] * len(values),
        out_shape=[jax.ShapeDtypeStruct(v.shape, v.dtype) for v in values],
        input_output_aliases={i: i for i in range(len(values))},
        cost_estimate=cost(2**34, 2**25),
    )(*values)


def room():
    return pl.pallas_call(
        lambda ref: None,
        out_specs=pl.BlockSpec(memory_space=pl.ANY),
        out_shape=jax.ShapeDtypeStruct((1024, 1280), F32),
        cost_estimate=cost(64, 64),
    )()


def exchange(env):
    order = jnp.zeros((8, 128), F32)
    for done, starts in STEPS:
        if done:
            if "zB" in done:
                env["pair"] = jnp.concatenate([env["zA"], env["zB"]])
            held = sorted(set(done) | {MOVES[name][0] for name in starts} - {"w"})
            if "zF" in done:
                held.append("room")
            *values, order = gate(*(env[name] for name in held), order)
            env.update(zip(held, values))
        for name in starts:
            source, axis, step = MOVES[name]
            env[name] = (shift if axis == "zl" else turn)(env[source], axis, step)
    return env


def local(hidden, hidden_q, norm_gain, doc_ids, w_query, w_key, w_value):
    dp, tensor = lax.axis_index("dp"), lax.axis_index("tensor")
    zh, y, c = dp // 8, dp // 2 % 4, dp % 2
    x, zl = tensor // 2, tensor % 2
    sign = 1 - 2 * c

    keep, give = prepare(c.reshape(1), hidden_q, hidden)
    piece = jnp.concatenate([keep, shift(give, "c", 1)], 1)
    env = exchange({"w": w_query, "p": piece, "room": room()})

    gain = take(norm_gain.reshape(16, 2, 256), c, 1)
    steps = (("", 0), (".A", -sign), (".B", sign), (".F", 2))
    at = [c, tensor] + [(zh + dz) % 4 for _, dz in steps]
    for block, dz in (("p", 0), ("l", 1)):
        at += [(x + dx) % 4 * 2 + (zl + dz) % 2 for _, dx in steps]
    at = jnp.stack(at + [(y + dy) % 4 for _, dy in steps] + [zl])
    rows = [env[block + name] for block in ("w", "pair", "zF") for name, _ in steps]
    pieces = [env[block + name] for block in ("p", "l") for name, _ in steps]

    w_key = w_key.reshape(4, 4, 2, 256, HS)
    w_value = w_value.reshape(4, 4, 2, 256, HS)
    early = project_early(
        at, pieces[:7], rows[:8], w_key, w_value, gain, env["room"]
    )
    own_rows, sib_rows, lead, scale = project(at, pieces, rows, w_key, w_value, gain, early)
    got_rows = shift(sib_rows, "c", 1).reshape(2, 2, LEN, 1280)
    got_lead = shift(lead, "c", 1)
    own_rows = own_rows.reshape(2, 2, LEN, 1280)
    scales = scale[:512].reshape(2, 2, LEN, HS)
    tables = rope_tables()
    place = jnp.stack([c, zh, y, tensor])
    att_q = attend(own_rows, got_rows, scales, doc_ids, tables)
    att_sib = shift(att_q, "c", 1)
    lead, att_q = lax.optimization_barrier((lead, att_q))
    band = band_moments(place, gain, lead, got_lead, scale, env["p"])
    keep, give = attend_diff(c.reshape(1), own_rows, got_rows, scales, doc_ids, tables, att_q)
    keep_sib = shift(give, "c", 1)
    here = {"zh": zh, "y": y}
    outs = []
    for left, left_sib, axis, other, more in (
        (keep, keep_sib, "zh", "y", ()),
        (att_q, att_sib, "y", "zh", (band,)),
    ):
        sums = moments(int(axis == "y"), place, left, left_sib, att_q, att_sib, *more)
        total = sums[0].astype(F32)
        for step in (2, 1, 3):
            total = total + shift(sums[step], axis, step).astype(F32)
        outs.append(scatter(total.astype(BF), other, here[other]) / TOKENS)
    head_delta, head_gram = outs

    band = head_gram[32:].reshape(2, 8, 2, 2, 256).transpose(2, 0, 1, 3, 4)
    other = shift(take(band, 1 - c, 1), "c", 1)
    mine = take(band, c, 1)
    band = jnp.stack(
        [jnp.where(c == 0, mine, other), jnp.where(c == 0, other, mine)], 3
    ).reshape(2, 8, WIDTH)
    return band[0], band[1], head_gram[None, :32], head_delta[None]


def solution(mesh):
    return jax.shard_map(
        local,
        mesh=mesh,
        in_specs=(
            P("dp", "tensor"),
            P("dp", "tensor"),
            P(),
            P("dp", None),
            P("dp", "tensor"),
            P(None, "tensor"),
            P(None, "tensor"),
        ),
        out_specs=(
            P("dp", "tensor"),
            P("dp", "tensor"),
            P("tensor", "dp", None),
            P("tensor", "dp", None),
        ),
        check_vma=False,
    )
```

```python
import functools

import functools

import jax
import jax.numpy as jnp
from jax import lax
from jax.experimental import pallas as pl
from jax.experimental.pallas import tpu as pltpu
from jax.sharding import PartitionSpec as P

HS = 128
QH = 8
LEN = 128
BAND = 256
WIDTH = 1024
TOKENS = 8192
EPS = 1e-05
ROPE_BASE = 500000.0
BF = jnp.bfloat16
F32 = jnp.float32

SIZES = {"zh": 4, "y": 4, "c": 2, "x": 4, "zl": 2}
STRIDES = {"zh": 64, "y": 16, "c": 8, "x": 2, "zl": 1}


def shift(value, axis, step):
    size, stride = SIZES[axis], STRIDES[axis]
    pairs = []
    for index in range(256):
        at = index // stride % size
        pairs.append((index, index + ((at + step) % size - at) * stride))
    return lax.ppermute(value, ("dp", "tensor"), pairs)


def turn(value, axis, step):
    size, stride = SIZES[axis], STRIDES[axis]
    pairs = []
    for index in range(256):
        at = index // stride % size
        own = -step if index // STRIDES["c"] % 2 else step
        pairs.append((index, index + ((at + own) % size - at) * stride))
    return lax.ppermute(value, ("dp", "tensor"), pairs)


def take(value, index, axis):
    return lax.dynamic_index_in_dim(value, index, axis, keepdims=False)


def params(mib):
    return pltpu.CompilerParams(vmem_limit_bytes=mib * 2**20)


def cost(flops, moved):
    return pl.CostEstimate(flops=flops, bytes_accessed=moved, transcendentals=0)


def apart(value):
    return pltpu.with_memory_space_constraint(value, pltpu.HBM)


def prepare_kernel(core, q_ref, f_ref, gain_ref, keep_ref, give_ref):
    first = core[0] == 0
    ones = jnp.ones((8, WIDTH), BF)
    nt = (((1,), (1,)), ((), ()))
    terms = []
    for stream, ref in enumerate((q_ref, f_ref)):
        square = jnp.square(ref[...].astype(F32))
        high = square.astype(BF)
        low = (square - high.astype(F32)).astype(BF)
        total = lax.dot_general(ones, high, nt, preferred_element_type=F32)
        total += lax.dot_general(ones, low, nt, preferred_element_type=F32)
        for _ in range(3):
            term = total[:1].astype(BF).astype(F32)
            terms.append(term)
            total = total - term
        for part in range(2):
            even, odd = (
                (ref[:, cols].astype(F32) * gain_ref[:, cols]).astype(BF)
                for cols in (pl.ds(512 * part + 256 * k, 256) for k in range(2))
            )
            rows = pl.ds(256 * stream, 256)
            keep_ref[part, rows] = jnp.where(first, even, odd)
            give_ref[part, rows] = jnp.where(first, odd, even)
    extra = jnp.concatenate(terms + [jnp.zeros((10, 256), F32)], axis=0).astype(BF)
    for part in range(2):
        keep_ref[part, pl.ds(512, 16)] = extra
        give_ref[part, pl.ds(512, 16)] = extra


def prepare(core, hidden_q, hidden, gain):
    out = pl.BlockSpec((2, 528, 256), lambda i, c: (0, 0, 0))
    return pl.pallas_call(
        prepare_kernel,
        grid_spec=pltpu.PrefetchScalarGridSpec(
            num_scalar_prefetch=1,
            grid=(1,),
            in_specs=[
                pl.BlockSpec((256, WIDTH), lambda i, c: (0, 0)),
                pl.BlockSpec((256, WIDTH), lambda i, c: (0, 0)),
                pl.BlockSpec((1, WIDTH), lambda i, c: (0, 0)),
            ],
            out_specs=[out, out],
        ),
        out_shape=[jax.ShapeDtypeStruct((2, 528, 256), BF)] * 2,
        compiler_params=params(16),
        cost_estimate=cost(0, 2**21),
    )(core, apart(hidden_q), apart(hidden), gain)


def early_kernel(at, *refs):
    s_refs, w_refs = refs[:7], refs[7:15]
    k_ref, v_ref, _, sums_ref, s_buf, w_buf, k_buf, v_buf, out_ref, s_sem, w_sem, kv_sem = refs[15:]
    k_copy = pltpu.make_async_copy(k_ref.at[:, :, at[0]], k_buf, kv_sem.at[0])
    v_copy = pltpu.make_async_copy(v_ref.at[:, :, at[0]], v_buf, kv_sem.at[1])
    s_copies, w_copies = [], []
    for index, ref in enumerate(s_refs):
        for half in range(2):
            source = ref.at[:, pl.ds(528 * half, 512)]
            target = s_buf.at[at[6 + index], :, pl.ds(512 * half, 512)]
            s_copies.append(pltpu.make_async_copy(source, target, s_sem.at[2 * index + half]))
    for group in range(3):
        for step in range(4):
            ref = w_refs[(0, 4, 4)[group] + step]
            rows = ref.at[pl.ds(256 if group == 2 else 0, 256)]
            target = w_buf.at[group, at[14 + step]]
            w_copies.append(pltpu.make_async_copy(rows, target, w_sem.at[4 * group + step]))
    for copy in s_copies + w_copies[:4] + [k_copy, v_copy] + w_copies[4:]:
        copy.start()
    for copy in s_copies:
        copy.wait()
    for group in range(3):
        for step in range(4):
            w_copies[4 * group + step].wait()
        if group == 0:
            k_copy.wait()
            v_copy.wait()
        place = at[2 + group]

        def add(first, count):
            rows = pl.ds(0, 1024)
            wide, narrow = block_product(
                s_buf, w_buf.at[group], k_buf, v_buf, place, first, count, rows
            )
            if group == 0:
                out_ref[:, :WIDTH] = wide
                out_ref[:, WIDTH:] = narrow
            else:
                out_ref[:, :WIDTH] += wide
                out_ref[:, WIDTH:] += narrow

        @pl.when(2 * place + 1 - at[18] != at[13])
        def _():
            add(0, 2)

        @pl.when(2 * place + 1 - at[18] == at[13])
        def _():
            add(at[18], 1)

    copy = pltpu.make_async_copy(out_ref, sums_ref, kv_sem.at[2])
    copy.start()
    copy.wait()


def block_product(s_buf, w_ref, k_buf, v_buf, place, first, count, rows):
    parts = []
    for step in range(count):
        slot = 2 * place + first + step
        for part in range(2):
            parts.append(s_buf[slot, part, rows, :])
    s = jnp.concatenate(parts, axis=1)
    blocks = pl.ds(2 * first, 2 * count)
    depth = 512 * count
    kv = jnp.concatenate(
        [ref[place, blocks].reshape(depth, HS) for ref in (k_buf, v_buf)], axis=1
    )
    wide = jnp.dot(s, w_ref[blocks].reshape(depth, WIDTH), preferred_element_type=F32)
    return wide, jnp.dot(s, kv, preferred_element_type=F32)


def final_kernel(at, *refs):
    s_refs, w_refs = refs[:8], refs[8:20]
    k_ref, v_ref, early_ref, out_ref, sib_ref, lead_ref, scale_ref = refs[20:27]
    s_buf, w_buf, k_buf, v_buf, sq_buf, lead_buf, acc, s_sem, w_sem, kv_sem, sq_sem = refs[27:]
    last, place = at[13], at[5]
    copies = []
    for index, ref in enumerate(s_refs):
        for half in range(2):
            rows = ref.at[0, pl.ds(528 * half + 512, 16)]
            target = sq_buf.at[half, index]
            copies.append(pltpu.make_async_copy(rows, target, sq_sem.at[2 * index + half]))
            copies[-1].start()
    k_copy = pltpu.make_async_copy(k_ref.at[:, :, at[0]], k_buf, kv_sem.at[0])
    v_copy = pltpu.make_async_copy(v_ref.at[:, :, at[0]], v_buf, kv_sem.at[1])
    early_copy = pltpu.make_async_copy(early_ref, acc, kv_sem.at[2])
    k_copy.start()
    v_copy.start()
    wanted = []
    for index, ref in enumerate(s_refs):
        slot = at[6 + index]
        for half in range(2):
            rows, target = pl.ds(528 * half, 512), pl.ds(512 * half, 512)
            sem = 2 * index + half
            copy = pltpu.make_async_copy(ref.at[:, rows], s_buf.at[slot, :, target], s_sem.at[sem])
            wanted.append(((slot // 2 == place) | (slot == last), copy))
            copy = pltpu.make_async_copy(ref.at[0, rows], lead_buf.at[target], sq_sem.at[16 + sem])
            wanted.append((slot == 0, copy))
    for step in range(4):
        target = w_buf.at[1, at[14 + step]]
        copy = pltpu.make_async_copy(w_refs[8 + step], target, w_sem.at[12 + step])
        wanted.append((at[0] >= 0, copy))
        for group in range(3):
            ref = w_refs[(0, 4, 4)[group] + step]
            rows = ref.at[pl.ds(256 if group == 2 else 0, 256)]
            target = w_buf.at[0, at[14 + step]]
            copy = pltpu.make_async_copy(rows, target, w_sem.at[4 * group + step])
            wanted.append((2 * at[2 + group] + 1 - at[18] == last, copy))
    for needed, copy in wanted:
        pl.when(needed)(copy.start)
    early_copy.start()

    for copy in copies:
        copy.wait()
    scales = []
    for half in range(2):
        squares = jnp.zeros((16, 256), F32)
        for index in range(8):
            squares += sq_buf[half, index].astype(F32)
        for first in (0, 3):
            square = squares[first : first + 1] + squares[first + 1 : first + 2]
            scale = lax.rsqrt((square + squares[first + 2 : first + 3]) / 8192.0 + EPS)
            scales.append(jnp.broadcast_to(scale, (128, 256)).T)
    scale = jnp.concatenate(scales, axis=0)
    scale_ref[...] = scale
    k_copy.wait()
    v_copy.wait()
    for needed, copy in wanted:
        pl.when(needed)(copy.wait)
    lead = lead_buf[...].astype(F32) * jnp.concatenate([scale, scale], axis=1)
    lead_ref[...] = lead.astype(BF)

    everything = pl.ds(0, 1024)
    wide, narrow = block_product(
        s_buf, w_buf.at[1], k_buf, v_buf, place, 0, 2, everything
    )
    early_copy.wait()
    acc[:, :WIDTH] += wide
    acc[:, WIDTH:] += narrow

    @pl.when(last // 2 != place)
    def _():
        wide, narrow = block_product(
            s_buf, w_buf.at[0], k_buf, v_buf, last // 2, 1 - at[18], 1, everything
        )
        acc[:, :WIDTH] += wide
        acc[:, WIDTH:] += narrow

    out_ref[...] = acc[:512]
    sib_ref[...] = acc[512:].astype(BF)


def whole(*shape):
    return pl.BlockSpec(shape, lambda i, at: (0,) * len(shape))


def project_early(at, pieces, rows, w_key, w_value, room):
    return pl.pallas_call(
        early_kernel,
        grid_spec=pltpu.PrefetchScalarGridSpec(
            num_scalar_prefetch=1,
            grid=(1,),
            in_specs=[pl.BlockSpec(memory_space=pltpu.HBM)] * 17
            + [pl.BlockSpec(memory_space=pltpu.HBM)],
            out_specs=pl.BlockSpec(memory_space=pltpu.HBM),
            scratch_shapes=[
                pltpu.VMEM((8, 2, 1024, 256), BF),
                pltpu.VMEM((3, 4, 256, WIDTH), BF),
                pltpu.VMEM((4, 4, 256, HS), BF),
                pltpu.VMEM((4, 4, 256, HS), BF),
                pltpu.VMEM((1024, 1280), F32),
                pltpu.SemaphoreType.DMA((14,)),
                pltpu.SemaphoreType.DMA((12,)),
                pltpu.SemaphoreType.DMA((3,)),
            ],
        ),
        out_shape=jax.ShapeDtypeStruct((1024, 1280), F32),
        input_output_aliases={18: 0},
        compiler_params=params(40),
        cost_estimate=cost(2 * 1024 * 3072 * 1280, 24 * 2**20),
    )(at, *map(apart, pieces), *map(apart, rows), apart(w_key), apart(w_value), apart(room))


def project(at, pieces, rows, w_key, w_value, early):
    return pl.pallas_call(
        final_kernel,
        grid_spec=pltpu.PrefetchScalarGridSpec(
            num_scalar_prefetch=1,
            grid=(1,),
            in_specs=[pl.BlockSpec(memory_space=pltpu.HBM)] * 22
            + [pl.BlockSpec(memory_space=pl.ANY)],
            out_specs=[whole(512, 1280), whole(512, 1280), whole(1024, 256), whole(1024, 128)],
            scratch_shapes=[
                pltpu.VMEM((8, 2, 1024, 256), BF),
                pltpu.VMEM((2, 4, 256, WIDTH), BF),
                pltpu.VMEM((4, 4, 256, HS), BF),
                pltpu.VMEM((4, 4, 256, HS), BF),
                pltpu.VMEM((2, 8, 16, 256), BF),
                pltpu.VMEM((1024, 256), BF),
                pltpu.VMEM((1024, 1280), F32),
                pltpu.SemaphoreType.DMA((16,)),
                pltpu.SemaphoreType.DMA((16,)),
                pltpu.SemaphoreType.DMA((3,)),
                pltpu.SemaphoreType.DMA((32,)),
            ],
        ),
        out_shape=[
            jax.ShapeDtypeStruct((512, 1280), F32),
            jax.ShapeDtypeStruct((512, 1280), BF),
            jax.ShapeDtypeStruct((1024, 256), BF),
            jax.ShapeDtypeStruct((1024, 128), F32),
        ],
        compiler_params=params(36),
        cost_estimate=cost(2 * 1024 * 1280 * 1280, 20 * 2**20),
    )(at, *map(apart, pieces), *map(apart, rows), apart(w_key), apart(w_value), apart(early))


def rope_tables():
    half = HS // 2
    frequency = ROPE_BASE ** (-jnp.arange(half, dtype=F32) * 2.0 / HS)
    angles = jnp.arange(LEN, dtype=F32)[:, None] * frequency[None, :]
    cosine, sine = jnp.cos(angles), jnp.sin(angles)
    return jnp.concatenate([cosine, cosine], 1), jnp.concatenate([-sine, sine], 1)


def attended_columns(own_ref, got_ref, scale_ref, col_ref, row_ref, cos_ref, sin_ref):
    cosine, sine = cos_ref[...], sin_ref[...]

    def columns(at):
        cols = pl.ds(at * HS, HS)
        total = own_ref[0, 0, :, cols] + got_ref[0, 0, :, cols].astype(F32)
        return total * scale_ref[0, 0]

    def rotate(block):
        return (block * cosine + pltpu.roll(block, HS // 2, 1) * sine).astype(BF)

    keys = rotate(columns(QH))
    values = columns(QH + 1).astype(BF)
    row = lax.broadcasted_iota(jnp.int32, (LEN, LEN), 0)
    col = lax.broadcasted_iota(jnp.int32, (LEN, LEN), 1)
    allowed = (col_ref[0] == row_ref[0]) & (col <= row)
    nt = (((1,), (1,)), ((), ()))
    queries = jnp.concatenate([rotate(columns(head)) for head in range(QH)], axis=0)
    scores = lax.dot_general(queries, keys, nt, preferred_element_type=F32) * HS ** (-0.5)
    scores = jnp.where(jnp.concatenate([allowed] * QH, axis=0), scores, -1e30)
    exponent = jnp.exp(scores - jnp.max(scores, axis=-1, keepdims=True))
    weights = (exponent / jnp.sum(exponent, axis=-1, keepdims=True)).astype(BF)
    attended = lax.dot_general(
        values, weights, (((0,), (1,)), ((), ())), preferred_element_type=F32
    ).astype(BF)
    return [attended[:, head * LEN : (head + 1) * LEN] for head in range(QH)]


def attend_kernel(own_ref, got_ref, scale_ref, col_ref, row_ref, cos_ref, sin_ref, out_ref):
    blocks = attended_columns(own_ref, got_ref, scale_ref, col_ref, row_ref, cos_ref, sin_ref)
    for head, block in enumerate(blocks):
        out_ref[pl.ds(head * HS, HS), :] = block


def attend_diff_kernel(
    core, own_ref, got_ref, scale_ref, col_ref, row_ref, cos_ref, sin_ref, q_ref, keep_ref, give_ref
):
    blocks = attended_columns(own_ref, got_ref, scale_ref, col_ref, row_ref, cos_ref, sin_ref)
    first = core[0] == 0
    for head, block in enumerate(blocks):
        diff = block.astype(F32) - q_ref[pl.ds(head * HS, HS), :].astype(F32)
        diff = diff.reshape(2, 2, 32, LEN)
        keep_ref[pl.ds(head * 2, 2)] = jnp.where(first, diff[:, 0], diff[:, 1]).astype(BF)
        give_ref[pl.ds(head * 2, 2)] = jnp.where(first, diff[:, 1], diff[:, 0]).astype(BF)


def attend(own_rows, got_rows, scale, ids, tables):
    rows = pl.BlockSpec((1, 1, LEN, 1280), lambda s: (0, s, 0, 0))
    scales = pl.BlockSpec((1, 1, LEN, HS), lambda s: (0, s, 0, 0))
    table = pl.BlockSpec((LEN, HS), lambda s: (0, 0))
    return pl.pallas_call(
        attend_kernel,
        grid=(2,),
        in_specs=[
            rows,
            rows,
            scales,
            pl.BlockSpec((1, LEN, 1), lambda s: (s, 0, 0)),
            pl.BlockSpec((1, 1, LEN), lambda s: (s, 0, 0)),
            table,
            table,
        ],
        out_specs=pl.BlockSpec((WIDTH, LEN), lambda s: (0, s)),
        out_shape=jax.ShapeDtypeStruct((WIDTH, 256), BF),
        compiler_params=params(16),
        cost_estimate=cost(2**27, 2**21),
    )(own_rows, got_rows, scale, ids[:, :, None], ids[:, None, :], *tables)


def attend_diff(core, own_rows, got_rows, scale, ids, tables, att_q):
    rows = pl.BlockSpec((1, 1, LEN, 1280), lambda s, c: (1, s, 0, 0))
    scales = pl.BlockSpec((1, 1, LEN, HS), lambda s, c: (1, s, 0, 0))
    table = pl.BlockSpec((LEN, HS), lambda s, c: (0, 0))
    half = pl.BlockSpec((16, 32, LEN), lambda s, c: (0, 0, s))
    return pl.pallas_call(
        attend_diff_kernel,
        grid_spec=pltpu.PrefetchScalarGridSpec(
            num_scalar_prefetch=1,
            grid=(2,),
            in_specs=[
                rows,
                rows,
                scales,
                pl.BlockSpec((1, LEN, 1), lambda s, c: (s, 0, 0)),
                pl.BlockSpec((1, 1, LEN), lambda s, c: (s, 0, 0)),
                table,
                table,
                pl.BlockSpec((WIDTH, LEN), lambda s, c: (0, s)),
            ],
            out_specs=[half, half],
        ),
        out_shape=[jax.ShapeDtypeStruct((16, 32, 256), BF)] * 2,
        compiler_params=params(16),
        cost_estimate=cost(2**27, 2**21),
    )(core, own_rows, got_rows, scale, ids[:, :, None], ids[:, None, :], *tables, att_q)


def moments_kernel(axis, place, left_ref, left_sib_ref, right_ref, right_sib_ref, *refs):
    nt = (((1,), (1,)), ((), ()))
    out_ref = refs[-1]

    def rows(ref):
        parts = []
        for step in range(4):
            near = (place[1 + axis] + step) % 4
            part = ref[:, near, 0] if axis else ref[near, :, 0]
            parts.append(part.reshape(128, 256))
        return jnp.concatenate(parts, axis=0)

    total = lax.dot_general(rows(left_ref), right_ref[...], nt, preferred_element_type=F32)
    total += lax.dot_general(
        rows(left_sib_ref), right_sib_ref[...], nt, preferred_element_type=F32
    )
    out_ref[:, :, :32] = total.astype(BF).reshape(4, 4, 32, WIDTH)
    if len(refs) == 2:
        for step in range(4):
            out_ref[step, :, 32:] = refs[0][:, (place[2] + step) % 4]


def moments(axis, place, left, left_sib, right, right_sib, *more):
    def side(value):
        if value.shape[0] == 16:
            value = value.reshape(4, 4, 1, 32, 256)
            return value, pl.BlockSpec((4, 4, 1, 32, 256), lambda i, p: (0, 0, 0, 0, 0))
        value = value.reshape(4, 4, 2, 32, 256)
        return value, pl.BlockSpec((4, 4, 1, 32, 256), lambda i, p: (0, 0, p[0], 0, 0))

    left, left_spec = side(left)
    left_sib, left_sib_spec = side(left_sib)
    whole = pl.BlockSpec((WIDTH, 256), lambda i, p: (0, 0))
    rows = 48 if more else 32
    return pl.pallas_call(
        functools.partial(moments_kernel, axis),
        grid_spec=pltpu.PrefetchScalarGridSpec(
            num_scalar_prefetch=1,
            grid=(1,),
            in_specs=[left_spec, left_sib_spec, whole, whole]
            + [pl.BlockSpec((4, 4, 16, WIDTH), lambda i, p: (0, 0, 0, 0))] * len(more),
            out_specs=pl.BlockSpec((4, 4, rows, WIDTH), lambda i, p: (0, 0, 0, 0)),
        ),
        out_shape=jax.ShapeDtypeStruct((4, 4, rows, WIDTH), BF),
        compiler_params=params(24),
        cost_estimate=cost(2**30, 2**21),
    )(place, left, left_sib, right, right_sib, *more)


def band_kernel(place, lead_ref, got_ref, scale_ref, piece_ref, out_ref):
    first = place[0] == 0
    tn = (((0,), (0,)), ((), ()))
    for part in range(2):
        gram = jnp.zeros((256, 256), F32)
        delta = jnp.zeros((256, 256), F32)
        for half in range(2):
            mine, theirs = pl.ds(512 * half, 512), pl.ds(512 - 512 * half, 512)
            lead = jnp.where(first, lead_ref[mine, :], got_ref[theirs, :])
            lead_q, lead_f = lead[:256], lead[256:]
            diff = (lead_f.astype(F32) - lead_q.astype(F32)).astype(BF)
            scale = scale_ref[pl.ds(512 * half, 256), :]
            right = piece_ref[part, pl.ds(528 * half, 256)].astype(F32)
            right = (right * jnp.concatenate([scale, scale], axis=1)).astype(BF)
            gram += lax.dot_general(lead_q, right, tn, preferred_element_type=F32)
            delta += lax.dot_general(diff, right, tn, preferred_element_type=F32)
        for index, value in enumerate((gram, delta)):
            cols = pl.ds(index * 512 + part * 256, 256)
            out_ref[:, :, :, cols] = value.astype(BF).reshape(4, 4, 16, 256)


def band_moments(place, *sides):
    return pl.pallas_call(
        band_kernel,
        in_specs=[pl.BlockSpec(memory_space=pltpu.SMEM)]
        + [pl.BlockSpec(memory_space=pltpu.VMEM)] * len(sides),
        out_specs=pl.BlockSpec(memory_space=pltpu.VMEM),
        out_shape=jax.ShapeDtypeStruct((4, 4, 16, WIDTH), BF),
        compiler_params=params(16),
        cost_estimate=cost(2**29, 2**21),
    )(place, *sides)


def scatter(parts, axis, here):
    total = take(parts, here, 0).astype(F32)
    for step in (1, 3, 2):
        total = total + shift(take(parts, (here + step) % 4, 0), axis, step).astype(F32)
    return total


MOVES = {
    "zA": ("w", "zh", 1),
    "zB": ("w", "zh", -1),
    "zF": ("zA", "zh", 1),
    "l": ("p", "zl", 1),
}
for block, axis in (("w", "y"), ("pair", "y"), ("zF", "y"), ("p", "x"), ("l", "x")):
    MOVES[block + ".A"] = (block, axis, 1)
    MOVES[block + ".B"] = (block, axis, -1)
    MOVES[block + ".F"] = (block + ".A", axis, 1)
MOVES["zF.F"] = ("zF", "y", 2)
STEPS = (
    ((), ("zA", "zB", "w.A", "w.B", "p.A")),
    (("zA", "zB", "w.A", "w.B", "p.A"), ("l", "pair.A", "pair.B", "p.B", "p.F")),
    (("l", "pair.A", "pair.B", "p.B", "p.F"), ("pair.F", "zF", "l.A", "l.B", "w.F")),
    (("pair.F", "zF"), ("zF.A", "zF.B", "zF.F")),
    (("l.A", "l.B", "w.F"), ("l.F",)),
    (("zF.A", "zF.B", "zF.F"), ()),
)


def gate(values, waited):
    count = len(values)
    return pl.pallas_call(
        lambda *refs: None,
        in_specs=[pl.BlockSpec(memory_space=pl.ANY)] * (count + len(waited)),
        out_specs=[pl.BlockSpec(memory_space=pl.ANY)] * count,
        out_shape=[jax.ShapeDtypeStruct(v.shape, v.dtype) for v in values],
        input_output_aliases={i: i for i in range(count)},
        cost_estimate=cost(2**34, 2**25),
    )(*values, *waited)


def room():
    return pl.pallas_call(
        lambda ref: None,
        out_specs=pl.BlockSpec(memory_space=pl.ANY),
        out_shape=jax.ShapeDtypeStruct((1024, 1280), F32),
        cost_estimate=cost(64, 64),
    )()


def exchange(env):
    order = jnp.zeros((8, 128), F32)
    for done, starts in STEPS:
        if done:
            if "zB" in done:
                env["pair"] = jnp.concatenate([env["zA"], env["zB"]])
            held = sorted({MOVES[name][0] for name in starts} - {"w"})
            if "l.A" in done:
                held += ["l.B"]
            if "zF" in done:
                held.append("room")
            if not starts:
                held += done
            waited = [env[name] for name in done if name not in held]
            *values, order = gate([env[name] for name in held] + [order], waited)
            env.update(zip(held, values))
        for name in starts:
            source, axis, step = MOVES[name]
            env[name] = (shift if axis == "zl" else turn)(env[source], axis, step)
    return env


def local(hidden, hidden_q, norm_gain, doc_ids, w_query, w_key, w_value):
    dp, tensor = lax.axis_index("dp"), lax.axis_index("tensor")
    zh, y, c = dp // 8, dp // 2 % 4, dp % 2
    x, zl = tensor // 2, tensor % 2
    sign = 1 - 2 * c

    gain = take(norm_gain.reshape(8, 1, WIDTH), tensor, 0)
    keep, give = prepare(c.reshape(1), hidden_q, hidden, gain)
    piece = jnp.concatenate([keep, shift(give, "c", 1)], 1)
    env = exchange({"w": w_query, "p": piece, "room": room()})

    steps = (("", 0), (".A", -sign), (".B", sign), (".F", 2))
    at = [c, tensor] + [(zh + dz) % 4 for _, dz in steps]
    for block, dz in (("p", 0), ("l", 1)):
        at += [(x + dx) % 4 * 2 + (zl + dz) % 2 for _, dx in steps]
    at = jnp.stack(at + [(y + dy) % 4 for _, dy in steps] + [zl])
    rows = [env[block + name] for block in ("w", "pair", "zF") for name, _ in steps]
    pieces = [env[block + name] for block in ("p", "l") for name, _ in steps]

    w_key = w_key.reshape(4, 4, 2, 256, HS)
    w_value = w_value.reshape(4, 4, 2, 256, HS)
    early = project_early(
        at, pieces[:7], rows[:8], w_key, w_value, env["room"]
    )
    own_rows, sib_rows, lead, scale = project(at, pieces, rows, w_key, w_value, early)
    got_rows = shift(sib_rows, "c", 1).reshape(2, 2, LEN, 1280)
    got_lead = shift(lead, "c", 1)
    own_rows = own_rows.reshape(2, 2, LEN, 1280)
    scales = scale[:512].reshape(2, 2, LEN, HS)
    tables = rope_tables()
    place = jnp.stack([c, zh, y, tensor])
    att_q = attend(own_rows, got_rows, scales, doc_ids, tables)
    att_sib = shift(att_q, "c", 1)
    lead, att_q = lax.optimization_barrier((lead, att_q))
    band = band_moments(place, lead, got_lead, scale, env["p"])
    keep, give = attend_diff(c.reshape(1), own_rows, got_rows, scales, doc_ids, tables, att_q)
    keep_sib = shift(give, "c", 1)
    here = {"zh": zh, "y": y}
    outs = []
    for left, left_sib, axis, other, more in (
        (keep, keep_sib, "zh", "y", ()),
        (att_q, att_sib, "y", "zh", (band,)),
    ):
        sums = moments(int(axis == "y"), place, left, left_sib, att_q, att_sib, *more)
        total = sums[0].astype(F32)
        for step in (2, 1, 3):
            total = total + shift(sums[step], axis, step).astype(F32)
        outs.append(scatter(total.astype(BF), other, here[other]) / TOKENS)
    head_delta, head_gram = outs

    band = head_gram[32:].reshape(2, 8, 2, 2, 256).transpose(2, 0, 1, 3, 4)
    other = shift(take(band, 1 - c, 1), "c", 1)
    mine = take(band, c, 1)
    band = jnp.stack(
        [jnp.where(c == 0, mine, other), jnp.where(c == 0, other, mine)], 3
    ).reshape(2, 8, WIDTH)
    return band[0], band[1], head_gram[None, :32], head_delta[None]


def solution(mesh):
    return jax.shard_map(
        local,
        mesh=mesh,
        in_specs=(
            P("dp", "tensor"),
            P("dp", "tensor"),
            P(),
            P("dp", None),
            P("dp", "tensor"),
            P(None, "tensor"),
            P(None, "tensor"),
        ),
        out_specs=(
            P("dp", "tensor"),
            P("dp", "tensor"),
            P("tensor", "dp", None),
            P("tensor", "dp", None),
        ),
        check_vma=False,
    )
```

```python
import functools

import functools

import jax
import jax.numpy as jnp
from jax import lax
from jax.experimental import pallas as pl
from jax.experimental.pallas import tpu as pltpu
from jax.sharding import PartitionSpec as P

HS = 128
QH = 8
LEN = 128
BAND = 256
WIDTH = 1024
TOKENS = 8192
EPS = 1e-05
ROPE_BASE = 500000.0
BF = jnp.bfloat16
F32 = jnp.float32

SIZES = {"zh": 4, "y": 4, "c": 2, "x": 4, "zl": 2}
STRIDES = {"zh": 64, "y": 16, "c": 8, "x": 2, "zl": 1}


def shift(value, axis, step):
    size, stride = SIZES[axis], STRIDES[axis]
    pairs = []
    for index in range(256):
        at = index // stride % size
        pairs.append((index, index + ((at + step) % size - at) * stride))
    return lax.ppermute(value, ("dp", "tensor"), pairs)


def turn(value, axis, step):
    size, stride = SIZES[axis], STRIDES[axis]
    pairs = []
    for index in range(256):
        at = index // stride % size
        own = -step if index // STRIDES["c"] % 2 else step
        pairs.append((index, index + ((at + own) % size - at) * stride))
    return lax.ppermute(value, ("dp", "tensor"), pairs)


def take(value, index, axis):
    return lax.dynamic_index_in_dim(value, index, axis, keepdims=False)


def params(mib):
    return pltpu.CompilerParams(vmem_limit_bytes=mib * 2**20)


def cost(flops, moved):
    return pl.CostEstimate(flops=flops, bytes_accessed=moved, transcendentals=0)


def apart(value):
    return pltpu.with_memory_space_constraint(value, pltpu.HBM)


def prepare_kernel(core, q_ref, f_ref, gain_ref, keep_ref, give_ref):
    first = core[0] == 0
    ones = jnp.ones((8, WIDTH), BF)
    nt = (((1,), (1,)), ((), ()))
    terms = []
    for stream, ref in enumerate((q_ref, f_ref)):
        square = jnp.square(ref[...].astype(F32))
        high = square.astype(BF)
        low = (square - high.astype(F32)).astype(BF)
        total = lax.dot_general(ones, high, nt, preferred_element_type=F32)
        total += lax.dot_general(ones, low, nt, preferred_element_type=F32)
        for _ in range(3):
            term = total[:1].astype(BF).astype(F32)
            terms.append(term)
            total = total - term
        for part in range(2):
            even, odd = (
                (ref[:, cols].astype(F32) * gain_ref[:, cols]).astype(BF)
                for cols in (pl.ds(512 * part + 256 * k, 256) for k in range(2))
            )
            rows = pl.ds(256 * stream, 256)
            keep_ref[part, rows] = jnp.where(first, even, odd)
            give_ref[part, rows] = jnp.where(first, odd, even)
    extra = jnp.concatenate(terms + [jnp.zeros((10, 256), F32)], axis=0).astype(BF)
    for part in range(2):
        keep_ref[part, pl.ds(512, 16)] = extra
        give_ref[part, pl.ds(512, 16)] = extra


def prepare(core, hidden_q, hidden, gain):
    out = pl.BlockSpec((2, 528, 256), lambda i, c: (0, 0, 0))
    return pl.pallas_call(
        prepare_kernel,
        grid_spec=pltpu.PrefetchScalarGridSpec(
            num_scalar_prefetch=1,
            grid=(1,),
            in_specs=[
                pl.BlockSpec((256, WIDTH), lambda i, c: (0, 0)),
                pl.BlockSpec((256, WIDTH), lambda i, c: (0, 0)),
                pl.BlockSpec((1, WIDTH), lambda i, c: (0, 0)),
            ],
            out_specs=[out, out],
        ),
        out_shape=[jax.ShapeDtypeStruct((2, 528, 256), BF)] * 2,
        compiler_params=params(16),
        cost_estimate=cost(0, 2**21),
    )(core, apart(hidden_q), apart(hidden), gain)


def early_kernel(at, *refs):
    s_refs, w_refs = refs[:7], refs[7:15]
    k_ref, v_ref, _, sums_ref, s_buf, w_buf, k_buf, v_buf, out_ref, s_sem, w_sem, kv_sem = refs[15:]
    k_copy = pltpu.make_async_copy(k_ref.at[:, :, at[0]], k_buf, kv_sem.at[0])
    v_copy = pltpu.make_async_copy(v_ref.at[:, :, at[0]], v_buf, kv_sem.at[1])
    s_copies, w_copies = [], []
    for index, ref in enumerate(s_refs):
        for half in range(2):
            source = ref.at[:, pl.ds(528 * half, 512)]
            target = s_buf.at[at[6 + index], :, pl.ds(512 * half, 512)]
            s_copies.append(pltpu.make_async_copy(source, target, s_sem.at[2 * index + half]))
    for group in range(3):
        for step in range(4):
            ref = w_refs[(0, 4, 4)[group] + step]
            rows = ref.at[pl.ds(256 if group == 2 else 0, 256)]
            target = w_buf.at[group, at[14 + step]]
            w_copies.append(pltpu.make_async_copy(rows, target, w_sem.at[4 * group + step]))
    for copy in s_copies + w_copies[:4] + [k_copy, v_copy] + w_copies[4:]:
        copy.start()
    for copy in s_copies:
        copy.wait()
    for group in range(3):
        for step in range(4):
            w_copies[4 * group + step].wait()
        if group == 0:
            k_copy.wait()
            v_copy.wait()
        place = at[2 + group]

        def add(first, count):
            rows = pl.ds(0, 1024)
            wide, narrow = block_product(
                s_buf, w_buf.at[group], k_buf, v_buf, place, first, count, rows
            )
            if group == 0:
                out_ref[:, :WIDTH] = wide
                out_ref[:, WIDTH:] = narrow
            else:
                out_ref[:, :WIDTH] += wide
                out_ref[:, WIDTH:] += narrow

        @pl.when(2 * place + 1 - at[18] != at[13])
        def _():
            add(0, 2)

        @pl.when(2 * place + 1 - at[18] == at[13])
        def _():
            add(at[18], 1)

    copy = pltpu.make_async_copy(out_ref, sums_ref, kv_sem.at[2])
    copy.start()
    copy.wait()


def block_product(s_buf, w_ref, k_buf, v_buf, place, first, count, rows):
    parts = []
    for step in range(count):
        slot = 2 * place + first + step
        for part in range(2):
            parts.append(s_buf[slot, part, rows, :])
    s = jnp.concatenate(parts, axis=1)
    blocks = pl.ds(2 * first, 2 * count)
    depth = 512 * count
    kv = jnp.concatenate(
        [ref[place, blocks].reshape(depth, HS) for ref in (k_buf, v_buf)], axis=1
    )
    wide = jnp.dot(s, w_ref[blocks].reshape(depth, WIDTH), preferred_element_type=F32)
    return wide, jnp.dot(s, kv, preferred_element_type=F32)


def final_kernel(at, *refs):
    s_refs, w_refs = refs[:8], refs[8:20]
    k_ref, v_ref, early_ref, out_ref, sib_ref, lead_ref, scale_ref = refs[20:27]
    s_buf, w_buf, k_buf, v_buf, sq_buf, lead_buf, acc, s_sem, w_sem, kv_sem, sq_sem = refs[27:]
    last, place = at[13], at[5]
    copies = []
    for index, ref in enumerate(s_refs):
        for half in range(2):
            rows = ref.at[0, pl.ds(528 * half + 512, 16)]
            target = sq_buf.at[half, index]
            copies.append(pltpu.make_async_copy(rows, target, sq_sem.at[2 * index + half]))
            copies[-1].start()
    k_copy = pltpu.make_async_copy(k_ref.at[:, :, at[0]], k_buf, kv_sem.at[0])
    v_copy = pltpu.make_async_copy(v_ref.at[:, :, at[0]], v_buf, kv_sem.at[1])
    early_copy = pltpu.make_async_copy(early_ref, acc, kv_sem.at[2])
    k_copy.start()
    v_copy.start()
    wanted = []
    for index, ref in enumerate(s_refs):
        slot = at[6 + index]
        for half in range(2):
            rows, target = pl.ds(528 * half, 512), pl.ds(512 * half, 512)
            sem = 2 * index + half
            copy = pltpu.make_async_copy(ref.at[:, rows], s_buf.at[slot, :, target], s_sem.at[sem])
            wanted.append(((slot // 2 == place) | (slot == last), copy))
            copy = pltpu.make_async_copy(ref.at[0, rows], lead_buf.at[target], sq_sem.at[16 + sem])
            wanted.append((slot == 0, copy))
    for step in range(4):
        target = w_buf.at[1, at[14 + step]]
        copy = pltpu.make_async_copy(w_refs[8 + step], target, w_sem.at[12 + step])
        wanted.append((at[0] >= 0, copy))
        for group in range(3):
            ref = w_refs[(0, 4, 4)[group] + step]
            rows = ref.at[pl.ds(256 if group == 2 else 0, 256)]
            target = w_buf.at[0, at[14 + step]]
            copy = pltpu.make_async_copy(rows, target, w_sem.at[4 * group + step])
            wanted.append((2 * at[2 + group] + 1 - at[18] == last, copy))
    for needed, copy in wanted:
        pl.when(needed)(copy.start)
    early_copy.start()

    for copy in copies:
        copy.wait()
    scales = []
    for half in range(2):
        squares = jnp.zeros((16, 256), F32)
        for index in range(8):
            squares += sq_buf[half, index].astype(F32)
        for first in (0, 3):
            square = squares[first : first + 1] + squares[first + 1 : first + 2]
            scale = lax.rsqrt((square + squares[first + 2 : first + 3]) / 8192.0 + EPS)
            scales.append(jnp.broadcast_to(scale, (128, 256)).T)
    scale = jnp.concatenate(scales, axis=0)
    scale_ref[...] = scale
    k_copy.wait()
    v_copy.wait()
    for needed, copy in wanted:
        pl.when(needed)(copy.wait)
    lead = lead_buf[...].astype(F32) * jnp.concatenate([scale, scale], axis=1)
    lead_ref[...] = lead.astype(BF)

    everything = pl.ds(0, 1024)
    wide, narrow = block_product(
        s_buf, w_buf.at[1], k_buf, v_buf, place, 0, 2, everything
    )
    early_copy.wait()
    acc[:, :WIDTH] += wide
    acc[:, WIDTH:] += narrow

    @pl.when(last // 2 != place)
    def _():
        wide, narrow = block_product(
            s_buf, w_buf.at[0], k_buf, v_buf, last // 2, 1 - at[18], 1, everything
        )
        acc[:, :WIDTH] += wide
        acc[:, WIDTH:] += narrow

    out_ref[...] = acc[:512]
    sib_ref[...] = acc[512:].astype(BF)


def whole(*shape):
    return pl.BlockSpec(shape, lambda i, at: (0,) * len(shape))


def project_early(at, pieces, rows, w_key, w_value, room):
    return pl.pallas_call(
        early_kernel,
        grid_spec=pltpu.PrefetchScalarGridSpec(
            num_scalar_prefetch=1,
            grid=(1,),
            in_specs=[pl.BlockSpec(memory_space=pltpu.HBM)] * 17
            + [pl.BlockSpec(memory_space=pltpu.HBM)],
            out_specs=pl.BlockSpec(memory_space=pltpu.HBM),
            scratch_shapes=[
                pltpu.VMEM((8, 2, 1024, 256), BF),
                pltpu.VMEM((3, 4, 256, WIDTH), BF),
                pltpu.VMEM((4, 4, 256, HS), BF),
                pltpu.VMEM((4, 4, 256, HS), BF),
                pltpu.VMEM((1024, 1280), F32),
                pltpu.SemaphoreType.DMA((14,)),
                pltpu.SemaphoreType.DMA((12,)),
                pltpu.SemaphoreType.DMA((3,)),
            ],
        ),
        out_shape=jax.ShapeDtypeStruct((1024, 1280), F32),
        input_output_aliases={18: 0},
        compiler_params=params(40),
        cost_estimate=cost(2 * 1024 * 3072 * 1280, 24 * 2**20),
    )(at, *map(apart, pieces), *map(apart, rows), apart(w_key), apart(w_value), apart(room))


def project(at, pieces, rows, w_key, w_value, early):
    return pl.pallas_call(
        final_kernel,
        grid_spec=pltpu.PrefetchScalarGridSpec(
            num_scalar_prefetch=1,
            grid=(1,),
            in_specs=[pl.BlockSpec(memory_space=pltpu.HBM)] * 22
            + [pl.BlockSpec(memory_space=pl.ANY)],
            out_specs=[whole(512, 1280), whole(512, 1280), whole(1024, 256), whole(1024, 128)],
            scratch_shapes=[
                pltpu.VMEM((8, 2, 1024, 256), BF),
                pltpu.VMEM((2, 4, 256, WIDTH), BF),
                pltpu.VMEM((4, 4, 256, HS), BF),
                pltpu.VMEM((4, 4, 256, HS), BF),
                pltpu.VMEM((2, 8, 16, 256), BF),
                pltpu.VMEM((1024, 256), BF),
                pltpu.VMEM((1024, 1280), F32),
                pltpu.SemaphoreType.DMA((16,)),
                pltpu.SemaphoreType.DMA((16,)),
                pltpu.SemaphoreType.DMA((3,)),
                pltpu.SemaphoreType.DMA((32,)),
            ],
        ),
        out_shape=[
            jax.ShapeDtypeStruct((512, 1280), F32),
            jax.ShapeDtypeStruct((512, 1280), BF),
            jax.ShapeDtypeStruct((1024, 256), BF),
            jax.ShapeDtypeStruct((1024, 128), F32),
        ],
        compiler_params=params(36),
        cost_estimate=cost(2 * 1024 * 1280 * 1280, 20 * 2**20),
    )(at, *map(apart, pieces), *map(apart, rows), apart(w_key), apart(w_value), apart(early))


def rope_tables():
    half = HS // 2
    frequency = ROPE_BASE ** (-jnp.arange(half, dtype=F32) * 2.0 / HS)
    angles = jnp.arange(LEN, dtype=F32)[:, None] * frequency[None, :]
    cosine, sine = jnp.cos(angles), jnp.sin(angles)
    return jnp.concatenate([cosine, cosine], 1), jnp.concatenate([-sine, sine], 1)


def attended_columns(own_ref, got_ref, scale_ref, col_ref, row_ref, cos_ref, sin_ref):
    cosine, sine = cos_ref[...], sin_ref[...]

    def columns(at):
        cols = pl.ds(at * HS, HS)
        total = own_ref[0, 0, :, cols] + got_ref[0, 0, :, cols].astype(F32)
        return total * scale_ref[0, 0]

    def rotate(block):
        return (block * cosine + pltpu.roll(block, HS // 2, 1) * sine).astype(BF)

    keys = rotate(columns(QH))
    values = columns(QH + 1).astype(BF)
    row = lax.broadcasted_iota(jnp.int32, (LEN, LEN), 0)
    col = lax.broadcasted_iota(jnp.int32, (LEN, LEN), 1)
    allowed = (col_ref[0] == row_ref[0]) & (col <= row)
    nt = (((1,), (1,)), ((), ()))
    queries = jnp.concatenate([rotate(columns(head)) for head in range(QH)], axis=0)
    scores = lax.dot_general(queries, keys, nt, preferred_element_type=F32) * HS ** (-0.5)
    scores = jnp.where(jnp.concatenate([allowed] * QH, axis=0), scores, -1e30)
    exponent = jnp.exp(scores - jnp.max(scores, axis=-1, keepdims=True))
    weights = (exponent / jnp.sum(exponent, axis=-1, keepdims=True)).astype(BF)
    attended = lax.dot_general(
        values, weights, (((0,), (1,)), ((), ())), preferred_element_type=F32
    ).astype(BF)
    return [attended[:, head * LEN : (head + 1) * LEN] for head in range(QH)]


def attend_kernel(own_ref, got_ref, scale_ref, col_ref, row_ref, cos_ref, sin_ref, out_ref):
    blocks = attended_columns(own_ref, got_ref, scale_ref, col_ref, row_ref, cos_ref, sin_ref)
    for head, block in enumerate(blocks):
        out_ref[pl.ds(head * HS, HS), :] = block


def attend_diff_kernel(
    core, own_ref, got_ref, scale_ref, col_ref, row_ref, cos_ref, sin_ref, q_ref, keep_ref, give_ref
):
    blocks = attended_columns(own_ref, got_ref, scale_ref, col_ref, row_ref, cos_ref, sin_ref)
    first = core[0] == 0
    for head, block in enumerate(blocks):
        diff = block.astype(F32) - q_ref[pl.ds(head * HS, HS), :].astype(F32)
        diff = diff.reshape(2, 2, 32, LEN)
        keep_ref[pl.ds(head * 2, 2)] = jnp.where(first, diff[:, 0], diff[:, 1]).astype(BF)
        give_ref[pl.ds(head * 2, 2)] = jnp.where(first, diff[:, 1], diff[:, 0]).astype(BF)


def attend(own_rows, got_rows, scale, ids, tables):
    rows = pl.BlockSpec((1, 1, LEN, 1280), lambda s: (0, s, 0, 0))
    scales = pl.BlockSpec((1, 1, LEN, HS), lambda s: (0, s, 0, 0))
    table = pl.BlockSpec((LEN, HS), lambda s: (0, 0))
    return pl.pallas_call(
        attend_kernel,
        grid=(2,),
        in_specs=[
            rows,
            rows,
            scales,
            pl.BlockSpec((1, LEN, 1), lambda s: (s, 0, 0)),
            pl.BlockSpec((1, 1, LEN), lambda s: (s, 0, 0)),
            table,
            table,
        ],
        out_specs=pl.BlockSpec((WIDTH, LEN), lambda s: (0, s)),
        out_shape=jax.ShapeDtypeStruct((WIDTH, 256), BF),
        compiler_params=params(16),
        cost_estimate=cost(2**27, 2**21),
    )(own_rows, got_rows, scale, ids[:, :, None], ids[:, None, :], *tables)


def attend_diff(core, own_rows, got_rows, scale, ids, tables, att_q):
    rows = pl.BlockSpec((1, 1, LEN, 1280), lambda s, c: (1, s, 0, 0))
    scales = pl.BlockSpec((1, 1, LEN, HS), lambda s, c: (1, s, 0, 0))
    table = pl.BlockSpec((LEN, HS), lambda s, c: (0, 0))
    half = pl.BlockSpec((16, 32, LEN), lambda s, c: (0, 0, s))
    return pl.pallas_call(
        attend_diff_kernel,
        grid_spec=pltpu.PrefetchScalarGridSpec(
            num_scalar_prefetch=1,
            grid=(2,),
            in_specs=[
                rows,
                rows,
                scales,
                pl.BlockSpec((1, LEN, 1), lambda s, c: (s, 0, 0)),
                pl.BlockSpec((1, 1, LEN), lambda s, c: (s, 0, 0)),
                table,
                table,
                pl.BlockSpec((WIDTH, LEN), lambda s, c: (0, s)),
            ],
            out_specs=[half, half],
        ),
        out_shape=[jax.ShapeDtypeStruct((16, 32, 256), BF)] * 2,
        compiler_params=params(16),
        cost_estimate=cost(2**27, 2**21),
    )(core, own_rows, got_rows, scale, ids[:, :, None], ids[:, None, :], *tables, att_q)


def moments_kernel(axis, place, left_ref, left_sib_ref, right_ref, right_sib_ref, *refs):
    nt = (((1,), (1,)), ((), ()))
    out_refs = refs[-4:]

    def rows(ref):
        parts = []
        for step in range(4):
            near = (place[1 + axis] + step) % 4
            part = ref[:, near, 0] if axis else ref[near, :, 0]
            parts.append(part.reshape(128, 256))
        return jnp.concatenate(parts, axis=0)

    total = lax.dot_general(rows(left_ref), right_ref[...], nt, preferred_element_type=F32)
    total += lax.dot_general(
        rows(left_sib_ref), right_sib_ref[...], nt, preferred_element_type=F32
    )
    for step, out_ref in enumerate(out_refs):
        out_ref[:, :32] = total[128 * step : 128 * step + 128].astype(BF).reshape(4, 32, WIDTH)
        if len(refs) == 5:
            out_ref[:, 32:] = refs[0][:, (place[2] + step) % 4]


def moments(axis, place, left, left_sib, right, right_sib, *more):
    def side(value):
        if value.shape[0] == 16:
            value = value.reshape(4, 4, 1, 32, 256)
            return value, pl.BlockSpec((4, 4, 1, 32, 256), lambda i, p: (0, 0, 0, 0, 0))
        value = value.reshape(4, 4, 2, 32, 256)
        return value, pl.BlockSpec((4, 4, 1, 32, 256), lambda i, p: (0, 0, p[0], 0, 0))

    left, left_spec = side(left)
    left_sib, left_sib_spec = side(left_sib)
    whole = pl.BlockSpec((WIDTH, 256), lambda i, p: (0, 0))
    rows = 48 if more else 32
    return pl.pallas_call(
        functools.partial(moments_kernel, axis),
        grid_spec=pltpu.PrefetchScalarGridSpec(
            num_scalar_prefetch=1,
            grid=(1,),
            in_specs=[left_spec, left_sib_spec, whole, whole]
            + [pl.BlockSpec((4, 4, 16, WIDTH), lambda i, p: (0, 0, 0, 0))] * len(more),
            out_specs=[pl.BlockSpec((4, rows, WIDTH), lambda i, p: (0, 0, 0))] * 4,
        ),
        out_shape=[jax.ShapeDtypeStruct((4, rows, WIDTH), BF)] * 4,
        compiler_params=params(24),
        cost_estimate=cost(2**30, 2**21),
    )(place, left, left_sib, right, right_sib, *more)


def band_kernel(place, lead_ref, got_ref, scale_ref, piece_ref, out_ref):
    first = place[0] == 0
    tn = (((0,), (0,)), ((), ()))
    for part in range(2):
        gram = jnp.zeros((256, 256), F32)
        delta = jnp.zeros((256, 256), F32)
        for half in range(2):
            mine, theirs = pl.ds(512 * half, 512), pl.ds(512 - 512 * half, 512)
            lead = jnp.where(first, lead_ref[mine, :], got_ref[theirs, :])
            lead_q, lead_f = lead[:256], lead[256:]
            diff = (lead_f.astype(F32) - lead_q.astype(F32)).astype(BF)
            scale = scale_ref[pl.ds(512 * half, 256), :]
            right = piece_ref[part, pl.ds(528 * half, 256)].astype(F32)
            right = (right * jnp.concatenate([scale, scale], axis=1)).astype(BF)
            gram += lax.dot_general(lead_q, right, tn, preferred_element_type=F32)
            delta += lax.dot_general(diff, right, tn, preferred_element_type=F32)
        for index, value in enumerate((gram, delta)):
            cols = pl.ds(index * 512 + part * 256, 256)
            out_ref[:, :, :, cols] = value.astype(BF).reshape(4, 4, 16, 256)


def band_moments(place, *sides):
    return pl.pallas_call(
        band_kernel,
        in_specs=[pl.BlockSpec(memory_space=pltpu.SMEM)]
        + [pl.BlockSpec(memory_space=pltpu.VMEM)] * len(sides),
        out_specs=pl.BlockSpec(memory_space=pltpu.VMEM),
        out_shape=jax.ShapeDtypeStruct((4, 4, 16, WIDTH), BF),
        compiler_params=params(16),
        cost_estimate=cost(2**29, 2**21),
    )(place, *sides)


def scatter(parts, axis, here):
    total = take(parts, here, 0).astype(F32)
    for step in (1, 3, 2):
        total = total + shift(take(parts, (here + step) % 4, 0), axis, step).astype(F32)
    return total


MOVES = {
    "zA": ("w", "zh", 1),
    "zB": ("w", "zh", -1),
    "zF": ("zA", "zh", 1),
    "l": ("p", "zl", 1),
}
for block, axis in (("w", "y"), ("pair", "y"), ("zF", "y"), ("p", "x"), ("l", "x")):
    MOVES[block + ".A"] = (block, axis, 1)
    MOVES[block + ".B"] = (block, axis, -1)
    MOVES[block + ".F"] = (block + ".A", axis, 1)
MOVES["zF.F"] = ("zF", "y", 2)
STEPS = (
    ((), ("zA", "zB", "w.A", "w.B", "p.A")),
    (("zA", "zB", "w.A", "w.B", "p.A"), ("l", "pair.A", "pair.B", "p.B", "p.F")),
    (("l", "pair.A", "pair.B", "p.B", "p.F"), ("pair.F", "zF", "l.A", "l.B", "w.F")),
    (("pair.F", "zF"), ("zF.A", "zF.B", "zF.F")),
    (("l.A", "l.B", "w.F"), ("l.F",)),
    (("zF.A", "zF.B", "zF.F"), ()),
)


def gate(values, waited):
    count = len(values)
    return pl.pallas_call(
        lambda *refs: None,
        in_specs=[pl.BlockSpec(memory_space=pl.ANY)] * (count + len(waited)),
        out_specs=[pl.BlockSpec(memory_space=pl.ANY)] * count,
        out_shape=[jax.ShapeDtypeStruct(v.shape, v.dtype) for v in values],
        input_output_aliases={i: i for i in range(count)},
        cost_estimate=cost(2**34, 2**25),
    )(*values, *waited)


def room():
    return pl.pallas_call(
        lambda ref: None,
        out_specs=pl.BlockSpec(memory_space=pl.ANY),
        out_shape=jax.ShapeDtypeStruct((1024, 1280), F32),
        cost_estimate=cost(64, 64),
    )()


def exchange(env):
    order = jnp.zeros((8, 128), F32)
    for done, starts in STEPS:
        if done:
            if "zB" in done:
                env["pair"] = jnp.concatenate([env["zA"], env["zB"]])
            held = sorted({MOVES[name][0] for name in starts} - {"w"})
            if "l.A" in done:
                held += ["l.B"]
            if "zF" in done:
                held.append("room")
            if not starts:
                held += done
            waited = [env[name] for name in done if name not in held]
            *values, order = gate([env[name] for name in held] + [order], waited)
            env.update(zip(held, values))
        for name in starts:
            source, axis, step = MOVES[name]
            env[name] = (shift if axis == "zl" else turn)(env[source], axis, step)
    return env


def local(hidden, hidden_q, norm_gain, doc_ids, w_query, w_key, w_value):
    dp, tensor = lax.axis_index("dp"), lax.axis_index("tensor")
    zh, y, c = dp // 8, dp // 2 % 4, dp % 2
    x, zl = tensor // 2, tensor % 2
    sign = 1 - 2 * c

    gain = take(norm_gain.reshape(8, 1, WIDTH), tensor, 0)
    keep, give = prepare(c.reshape(1), hidden_q, hidden, gain)
    piece = jnp.concatenate([keep, shift(give, "c", 1)], 1)
    env = exchange({"w": w_query, "p": piece, "room": room()})

    steps = (("", 0), (".A", -sign), (".B", sign), (".F", 2))
    at = [c, tensor] + [(zh + dz) % 4 for _, dz in steps]
    for block, dz in (("p", 0), ("l", 1)):
        at += [(x + dx) % 4 * 2 + (zl + dz) % 2 for _, dx in steps]
    at = jnp.stack(at + [(y + dy) % 4 for _, dy in steps] + [zl])
    rows = [env[block + name] for block in ("w", "pair", "zF") for name, _ in steps]
    pieces = [env[block + name] for block in ("p", "l") for name, _ in steps]

    w_key = w_key.reshape(4, 4, 2, 256, HS)
    w_value = w_value.reshape(4, 4, 2, 256, HS)
    early = project_early(
        at, pieces[:7], rows[:8], w_key, w_value, env["room"]
    )
    own_rows, sib_rows, lead, scale = project(at, pieces, rows, w_key, w_value, early)
    got_rows = shift(sib_rows, "c", 1).reshape(2, 2, LEN, 1280)
    got_lead = shift(lead, "c", 1)
    own_rows = own_rows.reshape(2, 2, LEN, 1280)
    scales = scale[:512].reshape(2, 2, LEN, HS)
    tables = rope_tables()
    place = jnp.stack([c, zh, y, tensor])
    att_q = attend(own_rows, got_rows, scales, doc_ids, tables)
    att_sib = shift(att_q, "c", 1)
    lead, att_q = lax.optimization_barrier((lead, att_q))
    band = band_moments(place, lead, got_lead, scale, env["p"])
    keep, give = attend_diff(c.reshape(1), own_rows, got_rows, scales, doc_ids, tables, att_q)
    keep_sib = shift(give, "c", 1)
    here = {"zh": zh, "y": y}
    outs = []
    for left, left_sib, axis, other, more in (
        (keep, keep_sib, "zh", "y", ()),
        (att_q, att_sib, "y", "zh", (band,)),
    ):
        sums = moments(int(axis == "y"), place, left, left_sib, att_q, att_sib, *more)
        total = sums[0].astype(F32)
        for step in (2, 1, 3):
            total = total + shift(sums[step], axis, step).astype(F32)
        outs.append(scatter(total.astype(BF), other, here[other]) / TOKENS)
    head_delta, head_gram = outs

    band = head_gram[32:].reshape(2, 8, 2, 2, 256).transpose(2, 0, 1, 3, 4)
    other = shift(take(band, 1 - c, 1), "c", 1)
    mine = take(band, c, 1)
    band = jnp.stack(
        [jnp.where(c == 0, mine, other), jnp.where(c == 0, other, mine)], 3
    ).reshape(2, 8, WIDTH)
    return band[0], band[1], head_gram[None, :32], head_delta[None]


def solution(mesh):
    return jax.shard_map(
        local,
        mesh=mesh,
        in_specs=(
            P("dp", "tensor"),
            P("dp", "tensor"),
            P(),
            P("dp", None),
            P("dp", "tensor"),
            P(None, "tensor"),
            P(None, "tensor"),
        ),
        out_specs=(
            P("dp", "tensor"),
            P("dp", "tensor"),
            P("tensor", "dp", None),
            P("tensor", "dp", None),
        ),
        check_vma=False,
    )
```
